768 devices in a mesh: slab: 96 (over z, y_hi, core), grp: 8 (over x, y_lo).
Axes of the slice: x: 4, y: 8 (y_hi: 4, y_lo: 2; y = y_hi * 2 + y_lo), z: 12, core: 2. Of those that a mesh axis runs over, the one named last changes fastest.
Arguments:
- positions: float32 [3, 49152], P(None, ('slab', 'grp')), may hold values from 0 to 2
- species: int32 [49152], P(('slab', 'grp')), may hold values from 0 to 3
- node_state: bfloat16 [49152, 128], P(('slab', 'grp')), may hold values from -6 to 6
- w_self: bfloat16 [128, 128], replicated, may hold values from -0.5 to 0.5
- w_send: bfloat16 [128, 128], replicated, may hold values from -0.5 to 0.5
- radial: float32 [8, 128], replicated, may hold values from -2 to 2
- w_mix: bfloat16 [128, 128], replicated, may hold values from -0.5 to 0.5
- readout: float32 [128], replicated, may hold values from -0.078125 to 0.078125
- pair_scale: float32 [4, 4], replicated, may hold values from 0.5 to 2
- nbr_blocks: int32 [768, 4], P(('slab', 'grp')), may hold values from 0 to 23, as said below
- tile_count: int32 [768], P(('slab', 'grp')), may hold values from 2 to 4
Outputs:
- atom_energy: float32 [49152], P(('slab', 'grp'))
- forces: float32 [3, 49152], P(None, ('slab', 'grp'))
The draws below stay inside these ranges and needn't reach their ends.
Inputs may be any that keep to these rules, and one draw needn't show every extreme that they name: `nbr_blocks`: in every row, entry 0 is below 8 (a block of the lower slab's group) and entry 1 is at least 2 * 8 (a block of the upper slab's group).
All inputs are finite; a program needn't handle non-finite values.
Results may differ from the reference program's by a relative error of at most 0.0022.
Values sent between devices are 32-bit elements; how exact they have to be, the bound alone decides.
A program may use at most 32 MiB of HBM per device.

```python
import math
import jax
import jax.numpy as jnp
from jax import lax

C = 128
NBASIS = 8
SPECIES = 4
BLOCK = 64
K = 4
NBLK = 1
NBLOCKS = 768
ATOMS = 49152
N_GRP = 8


def draw_nbr_blocks(key, part):
    key = jax.random.fold_in(key, 11)
    per_slab = N_GRP * NBLK
    anywhere = jax.random.randint(key, (NBLOCKS, K), 0, 3 * per_slab)
    lowest = jax.random.randint(jax.random.fold_in(key, 1), (NBLOCKS, 1), 0, per_slab)
    highest = jax.random.randint(jax.random.fold_in(key, 2), (NBLOCKS, 1), 2 * per_slab, 3 * per_slab)
    column = jnp.arange(K)[None, :]
    picked = jnp.where(column == 0, lowest, jnp.where(column == 1, highest, anywhere))
    return picked.astype(jnp.int32)


def place_ends(drawn, rng, low, high):
    place = [jax.random.randint(jax.random.fold_in(rng, axis), (), 0, length) for axis, length in enumerate(drawn.shape)]
    longest = drawn.shape.index(max(drawn.shape))
    next_to = place[:longest] + [(place[longest] + 1) % drawn.shape[longest]] + place[longest + 1:]
    return drawn.at[tuple(place)].set(low).at[tuple(next_to)].set(high)


def block_levels(stream_key, extent, shards, least, high):
    level = 1.0
    for dim, shards_of in shards:
        draws = jax.random.uniform(jax.random.fold_in(jax.random.fold_in(stream_key, 6), dim), (shards_of,), jnp.float32, least / len(shards), high / len(shards))
        level = level * jnp.repeat(jnp.exp(draws), extent[dim] // shards_of).reshape((-1,) + (1,) * (len(extent) - 1 - dim))
    return level


def scatter_about(stream_key, extent, spread, most, split=(), kind=jnp.bfloat16):
    entries = jax.random.normal(stream_key, extent, jnp.float32) * spread
    if len(split) > 0:
        entries = block_levels(stream_key, extent, split, -0.22, 0.18) * entries
    return jnp.clip(entries, min=-most, max=most).astype(kind)


def setup_inputs(seed: int = 0) -> dict:
    keys = jax.random.split(jax.random.key(seed), 12)
    return {
        "positions": jnp.clip(2.0 * jax.random.uniform(keys[0], (3, ATOMS), jnp.float32) ** block_levels(keys[0], (3, ATOMS), ((1, 768),), -0.2, 0.2), 0.0, 2.0),
        "species": place_ends(jax.random.randint(keys[1], (ATOMS,), 0, SPECIES), jax.random.fold_in(keys[1], 1), 0, SPECIES - 1).astype(jnp.int32),
        "node_state": scatter_about(keys[2], (ATOMS, C), 1.0, 6.0, ((0, 768),)),
        "w_self": scatter_about(keys[3], (C, C), C ** -0.5, 0.5),
        "w_send": scatter_about(keys[4], (C, C), C ** -0.5, 0.5),
        "radial": scatter_about(keys[5], (NBASIS, C), NBASIS ** -0.5, 2.0, (), jnp.float32),
        "w_mix": scatter_about(keys[6], (C, C), C ** -0.5, 0.5),
        "readout": scatter_about(keys[7], (C,), 0.005, 0.078125, (), jnp.float32),
        "pair_scale": jnp.clip(jnp.exp(jax.random.uniform(keys[8], (SPECIES, SPECIES), jnp.float32, math.log(0.5), math.log(2.0))), 0.5, 2.0),
        "nbr_blocks": draw_nbr_blocks(jax.random.fold_in(keys[11], 71), 0),
        "tile_count": place_ends(jax.random.randint(keys[10], (NBLOCKS,), 2, K + 1), jax.random.fold_in(keys[10], 1), 2, K).astype(jnp.int32),
    }


def pair_tile(pos_i, pos_j, spc_i, spc_j, self_i, send_j, keep, radial, w_mix, readout, pair_scale):
    diff = pos_j[:, None, :] - pos_i[:, :, None]
    dist_sq = lax.optimization_barrier(jnp.sum(diff * diff, axis=0))
    kinds = jnp.arange(pair_scale.shape[0]).astype(jnp.float32)
    onehot_i = (spc_i[:, None] == kinds[None, :]).astype(jnp.float32)
    onehot_j = (spc_j[:, None] == kinds[None, :]).astype(jnp.float32)
    scale = jnp.dot(jnp.dot(onehot_i, pair_scale, precision=lax.Precision.HIGHEST), onehot_j.T, precision=lax.Precision.HIGHEST)
    scaled = dist_sq * scale
    cutoff = jnp.maximum(1.0 - scaled / 2.5, 0.0) ** 2
    nbasis = radial.shape[0]
    spacing = 2.5 / (nbasis - 1)
    centers = jnp.arange(nbasis).astype(jnp.float32) * spacing
    basis = jnp.exp(-((scaled[:, :, None] - centers) / spacing) ** 2)
    atom_block_list = pos_i.shape[1]
    width = radial.shape[1]
    latent = self_i[:, None, :] + send_j[None, :, :] + jnp.einsum('ijm,mc->ijc', basis, radial, precision=lax.Precision.HIGHEST)
    hidden = jax.nn.silu(latent).astype(jnp.bfloat16).reshape(atom_block_list * atom_block_list, width)
    mixed = jax.nn.silu(jnp.dot(hidden, w_mix, preferred_element_type=jnp.float32))
    energy = jnp.dot(mixed, readout, precision=lax.Precision.HIGHEST).reshape(atom_block_list, atom_block_list)
    return energy * cutoff * keep

def tile_grads(pos_i, pos_j, spc_i, spc_j, self_i, send_j, keep, radial, w_mix, readout, pair_scale):

    def total(first, second):
        return pair_tile(first, second, spc_i, spc_j, self_i, send_j, keep, radial, w_mix, readout, pair_scale)
    pair, pullback = jax.vjp(total, pos_i, pos_j)
    grad_i, grad_j = pullback(jnp.ones_like(pair))
    return (lax.optimization_barrier(jnp.sum(pair, axis=1)), grad_i, grad_j)

def reference(positions, species, node_state, w_self, w_send, radial, w_mix, readout, pair_scale, nbr_blocks, tile_count):
    self_feat = jnp.dot(node_state, w_self, preferred_element_type=jnp.float32)
    sender_features = jnp.dot(node_state, w_send, preferred_element_type=jnp.float32)
    species_labels = species.astype(jnp.float32)
    per_slab = N_GRP * NBLK
    ident = jnp.eye(BLOCK, dtype=jnp.float32)

    def one_block(block):
        slab_no = block // per_slab
        global_ids = ((slab_no * per_slab - per_slab + nbr_blocks[block]) % NBLOCKS).astype(jnp.int32)
        start_i = (block * BLOCK).astype(jnp.int32)
        pos_i = lax.dynamic_slice_in_dim(positions, start_i, BLOCK, 1)
        spc_i = lax.dynamic_slice_in_dim(species_labels, start_i, BLOCK, 0)
        self_i = lax.dynamic_slice_in_dim(self_feat, start_i, BLOCK, 0)
        live = (jnp.arange(K) < tile_count[block]).astype(jnp.float32)

        def one_tile(other, alive):
            start_j = (other * BLOCK).astype(jnp.int32)
            pos_j = lax.dynamic_slice_in_dim(positions, start_j, BLOCK, 1)
            spc_j = lax.dynamic_slice_in_dim(species_labels, start_j, BLOCK, 0)
            send_j = lax.dynamic_slice_in_dim(sender_features, start_j, BLOCK, 0)
            keep = alive * jnp.where(other == block, 1.0 - ident, jnp.ones_like(ident))
            return tile_grads(pos_i, pos_j, spc_i, spc_j, self_i, send_j, keep, radial, w_mix, readout, pair_scale)
        sums, grad_i, grad_j = jax.vmap(one_tile)(global_ids, live)
        return (lax.optimization_barrier(jnp.sum(sums, axis=0)), lax.optimization_barrier(jnp.sum(grad_i, axis=0)), grad_j, global_ids)
    energies, grad_own, grad_far, targets = lax.map(one_block, jnp.arange(NBLOCKS).astype(jnp.int32))
    gathered = jnp.zeros((NBLOCKS, 3, BLOCK), jnp.float32).at[targets.reshape(-1)].add(grad_far.reshape(-1, 3, BLOCK))
    grad_all = grad_own + gathered
    forces = -jnp.transpose(grad_all, (1, 0, 2)).reshape(3, ATOMS)
    return (energies.reshape(ATOMS), forces)
```

```python
import functools

import jax
import jax.numpy as jnp
from jax import lax
from jax.experimental import pallas as pl
from jax.experimental.pallas import tpu as pltpu
from jax.sharding import PartitionSpec as P

BLOCK = 64
C = 128
ROWS = 72
PAIRS = BLOCK * BLOCK
CHUNK = 512
SPACING = 2.5 / 7
MESH = pl.DeviceIdType.MESH
BF16, F32 = jnp.bfloat16, jnp.float32


def parts(value, count):
    found = []
    for _ in range(count):
        part = value.astype(BF16).astype(F32)
        found.append(part)
        value = value - part
    return found


def dot(left, right):
    return jnp.dot(left, right, preferred_element_type=F32)


def centre_onehot(start, width):
    lane = lax.broadcasted_iota(jnp.int32, (BLOCK, width), 1) + start
    row = lax.broadcasted_iota(jnp.int32, (BLOCK, width), 0)
    return jnp.where((lane // BLOCK) == row, 1.0, 0.0).astype(F32)


def kernel(
    slabs,
    members,
    pos_ref,
    spc_ref,
    node_ref,
    wself_ref,
    wsend_ref,
    radial_ref,
    wmix_ref,
    readout_ref,
    scale_ref,
    nbr_ref,
    count_ref,
    energy_ref,
    force_ref,
    own,
    sib,
    far,
    cur,
    self_exp,
    pos_exp,
    scale_exp,
    rhs_tail,
    lhs_z,
    lhs_b,
    lhs_r,
    lhs_m,
    ro_exp,
    pair_acc,
    tile_acc,
    grads,
    back,
    send_sem,
    recv_sem,
    back_send_sem,
    back_recv_sem,
):
    slab, me = lax.axis_index("slab"), lax.axis_index("grp")
    core = lax.rem(slab, 2)
    sib_slab = slab + 1 - 2 * core
    far_slab = lax.rem(slab - 1 + 2 * core + slabs, slabs)
    sib_panel, far_panel = 2 - 2 * core, 2 * core

    barrier = pltpu.get_barrier_semaphore()
    for k in range(members):
        to = lax.rem(me + k, members)
        pl.semaphore_signal(barrier, inc=1, device_id=(sib_slab, to), device_id_type=MESH)
        pl.semaphore_signal(barrier, inc=1, device_id=(far_slab, to), device_id_type=MESH)
        if k:
            pl.semaphore_signal(barrier, inc=1, device_id=(slab, to), device_id_type=MESH)

    species = spc_ref[...].astype(F32).reshape(1, BLOCK)
    own[me, 0:BLOCK, :] = dot(node_ref[...], wsend_ref[...])
    pad = jnp.zeros((1, BLOCK), F32)
    place = jnp.concatenate([pos_ref[...], species, pad, pad, pad, pad], axis=0)
    own[me, BLOCK:ROWS, :] = jnp.concatenate([place, jnp.zeros_like(place)], axis=1)

    pl.semaphore_wait(barrier, 3 * members - 1)

    def send(panel, index, to_slab, to):
        pltpu.make_async_remote_copy(
            src_ref=own.at[me],
            dst_ref=panel.at[me],
            send_sem=send_sem,
            recv_sem=recv_sem.at[index],
            device_id=(to_slab, to),
            device_id_type=MESH,
        ).start()

    for k in range(members):
        send(sib, 0, sib_slab, lax.rem(me + k, members))
    for k in range(members):
        send(far, 1, far_slab, lax.rem(me + k, members))
    for k in range(1, members):
        send(own, 2, slab, lax.rem(me + k, members))

    row8 = lax.broadcasted_iota(jnp.int32, (8, BLOCK), 0)
    scale8 = jnp.zeros((8, BLOCK), F32)
    for r in range(4):
        for s in range(4):
            scale8 = jnp.where((row8 == s) & (species == float(r)), scale_ref[r, s], scale8)
    small = jnp.concatenate(parts(place, 3) + parts(scale8, 3), axis=0).astype(BF16)
    self_feat = dot(node_ref[...], wself_ref[...]) * 0.5
    self_t = jnp.concatenate(parts(self_feat, 2), axis=0).T.astype(BF16)

    def expand(step, carry):
        lanes = pl.ds(pl.multiple_of(step * CHUNK, CHUNK), CHUNK)
        hot = centre_onehot(step * CHUNK, CHUNK)
        spread = dot(small, hot.astype(BF16))
        pos_exp[:, lanes] = spread[0:8] + spread[8:16] + spread[16:24]
        scale_exp[:, lanes] = spread[24:32] + spread[32:40] + spread[40:48]
        self_exp[:, lanes] = dot(self_t, jnp.concatenate([hot, hot], axis=0).astype(BF16))
        return carry

    lax.fori_loop(0, PAIRS // CHUNK, expand, 0)

    atom = lax.broadcasted_iota(jnp.int32, (BLOCK, CHUNK), 0)
    lane = lax.broadcasted_iota(jnp.int32, (BLOCK, CHUNK), 1)
    hot_j = jnp.where(lax.rem(lane, BLOCK) == atom, 1.0, 0.0).astype(F32)
    rhs_tail[...] = jnp.concatenate([hot_j, hot_j], axis=0).astype(BF16)

    radial_hi, radial_lo = parts(radial_ref[...], 2)
    lhs_r[...] = (jnp.concatenate([radial_hi, radial_lo], axis=0) * 0.25).astype(BF16)
    lhs_m[...] = (wmix_ref[...].astype(F32).T * 0.5).astype(BF16)
    ones = jnp.ones((16, C), F32)
    lhs_b[...] = jnp.concatenate(
        [
            jnp.concatenate([jnp.zeros((C, C), F32), ones], axis=0),
            jnp.concatenate([wmix_ref[...].astype(F32), jnp.zeros((16, C), F32)], axis=0),
        ],
        axis=1,
    ).astype(BF16)
    readout = readout_ref[...].reshape(1, C)
    ro_exp[...] = jnp.broadcast_to(readout, (C, C)).T
    pair_acc[...] = jnp.zeros_like(pair_acc)
    grads[...] = jnp.zeros_like(grads)

    center = lax.broadcasted_iota(jnp.int32, (8, CHUNK), 0).astype(F32) * SPACING
    row = lax.broadcasted_iota(jnp.int32, (8, CHUNK), 0)
    pair = lax.broadcasted_iota(jnp.int32, (8, CHUNK), 1)

    def tile(turn, carry):
        slot = jnp.where(turn == 0, 1 - core, jnp.where(turn == 1, core, turn))
        other = nbr_ref[0, slot]
        panel, member = other // members, lax.rem(other, members)

        @pl.when(turn == 0)
        def _():
            pltpu.make_async_copy(sib, sib, recv_sem.at[0]).wait()
            cur[...] = sib[member]

        @pl.when(turn == 1)
        def _():
            pltpu.make_async_copy(far, far, recv_sem.at[1]).wait()
            cur[...] = far[member]

        @pl.when(turn == 2)
        def _():
            some = own.at[pl.ds(0, members - 1)]
            pltpu.make_async_copy(some, some, recv_sem.at[2]).wait()

        @pl.when(turn >= 2)
        def _():
            cur[...] = jnp.where(
                panel == sib_panel,
                sib[member],
                jnp.where(panel == far_panel, far[member], own[member]),
            )

        live = jnp.where(slot < count_ref[0], 1.0, 0.0)
        same = (panel == 1) & (member == me)
        place_j = cur[BLOCK:ROWS, 0:BLOCK]
        place_j = jnp.concatenate([place_j] * (CHUNK // BLOCK), axis=1)
        kind_j = jnp.broadcast_to(place_j[3:4], (8, CHUNK))
        kind_hot = jnp.where(kind_j == row.astype(F32), 1.0, 0.0)
        send_hi, send_lo = parts(cur[0:BLOCK, :] * 0.5, 2)
        half_hi, half_lo = parts(radial_ref[...] * 0.5, 2)
        lhs_z[...] = jnp.concatenate(
            [half_hi, half_lo, half_hi, jnp.zeros((8, C), F32), send_hi, send_lo], axis=0
        ).T.astype(BF16)
        tile_acc[...] = jnp.zeros_like(tile_acc)

        def step(index, carry):
            start = pl.multiple_of(index * CHUNK, CHUNK)
            lanes = pl.ds(start, CHUNK)
            diff = jnp.where(row < 3, place_j - pos_exp[:, lanes], 0.0)
            dist_sq = jnp.sum(diff * diff, axis=0, keepdims=True)
            scale = jnp.sum(scale_exp[:, lanes] * kind_hot, axis=0, keepdims=True)
            scaled = dist_sq * scale
            centre = (pair + start) // BLOCK
            keep = jnp.where(same & (centre == lax.rem(pair, BLOCK)), 0.0, live)[0:1]
            reach = jnp.maximum(1.0 - scaled / 2.5, 0.0)
            cut = reach * reach
            offset = (scaled - center) / SPACING
            basis = jnp.exp(-(offset * offset))
            slope = basis * offset * (-2.0 / SPACING)
            basis_hi, basis_lo = parts(basis, 2)
            head = jnp.concatenate(
                [basis_hi, basis_hi, basis_lo, jnp.zeros((8, CHUNK), F32)], axis=0
            ).astype(BF16)
            rhs = jnp.concatenate([head, rhs_tail[...]], axis=0)
            half = dot(lhs_z[...], rhs) + self_exp[:, lanes]
            t = jnp.tanh(half)
            p = 1.0 + t
            hidden = half * p
            slope_1 = p * (1.0 + half * (1.0 - t))
            half = dot(lhs_m[...], hidden.astype(BF16))
            t = jnp.tanh(half)
            p = (1.0 + t) * jnp.concatenate([ro_exp[...]] * (CHUNK // C), axis=1)
            mixed = half * p
            slope_2 = p * (1.0 + half * (1.0 - t))
            out = dot(lhs_b[...], jnp.concatenate([mixed, slope_2], axis=0).astype(BF16))
            d_latent = out[0:C] * slope_1
            d_basis = dot(lhs_r[...], d_latent.astype(BF16))
            d_basis = d_basis[0:8] + d_basis[8:16]
            energy = out[C : C + 1]
            d_scaled = cut * jnp.sum(d_basis * slope, axis=0, keepdims=True)
            d_scaled = d_scaled - (2.0 / 2.5) * reach * energy
            force = (2.0 * keep * scale * d_scaled) * diff
            found = jnp.where(row == 3, keep * cut * energy, force)
            pair_acc[:, lanes] += found
            total = found[:, 0:C]
            for k in range(1, CHUNK // C):
                total = total + found[:, k * C : (k + 1) * C]
            tile_acc[...] += total
            return carry

        lax.fori_loop(0, PAIRS // CHUNK, step, 0)
        grad = tile_acc[:, 0:BLOCK] + tile_acc[:, BLOCK:C]
        grad = jnp.concatenate([grad, jnp.zeros_like(grad)], axis=1)
        group = jnp.where(panel == sib_panel, 0, jnp.where(panel == far_panel, 1, 2))
        which = group * members + member
        for k in range(3 * members):
            grads[k] += jnp.where(which == k, grad, 0.0)
        return carry

    lax.fori_loop(0, 4, tile, 0)

    def give(index, to_slab, to):
        pltpu.make_async_remote_copy(
            src_ref=grads.at[index * members + to],
            dst_ref=back.at[index * members + me],
            send_sem=back_send_sem,
            recv_sem=back_recv_sem,
            device_id=(to_slab, to),
            device_id_type=MESH,
        ).start()

    for k in range(members):
        give(1, far_slab, lax.rem(me + k, members))
    for k in range(1, members):
        give(2, slab, lax.rem(me + k, members))
    for k in range(members):
        give(0, sib_slab, lax.rem(me + k, members))
    back[2 * members + me] = grads[2 * members + me]

    def gather(index, total):
        lanes = pl.ds(pl.multiple_of(index * CHUNK, CHUNK), CHUNK)
        split = jnp.concatenate(parts(pair_acc[:, lanes], 3), axis=0).astype(BF16)
        hot = centre_onehot(index * CHUNK, CHUNK).astype(BF16)
        found = lax.dot_general(
            split, hot, (((1,), (1,)), ((), ())), preferred_element_type=F32
        )
        return total + (found[0:8] + found[8:16] + found[16:24])

    centre_sum = lax.fori_loop(0, PAIRS // CHUNK, gather, jnp.zeros((8, BLOCK), F32))
    energy_ref[...] = centre_sum[3:4].reshape(BLOCK)

    some = back.at[pl.ds(0, 3 * members - 1)]
    pltpu.make_async_copy(some, some, back_recv_sem).wait()
    total = back[0]
    for k in range(1, 3 * members):
        total = total + back[k]
    force_ref[...] = centre_sum[0:3] - total[0:3, 0:BLOCK]

    for panel in (sib, far, own.at[pl.ds(0, members - 1)]):
        pltpu.make_async_copy(panel, panel, send_sem).wait()
    pltpu.make_async_copy(some, some, back_send_sem).wait()


def solution(mesh):
    slabs, members = mesh.shape["slab"], mesh.shape["grp"]
    vmem = pl.BlockSpec(memory_space=pltpu.VMEM)
    smem = pl.BlockSpec(memory_space=pltpu.SMEM)
    panel = pltpu.VMEM((members, ROWS, C), F32)
    call = pl.pallas_call(
        functools.partial(kernel, slabs, members),
        out_shape=(
            jax.ShapeDtypeStruct((BLOCK,), F32),
            jax.ShapeDtypeStruct((3, BLOCK), F32),
        ),
        in_specs=[vmem] * 8 + [smem] * 3,
        out_specs=(vmem, vmem),
        scratch_shapes=[
            panel,
            panel,
            panel,
            pltpu.VMEM((ROWS, C), F32),
            pltpu.VMEM((C, PAIRS), F32),
            pltpu.VMEM((8, PAIRS), F32),
            pltpu.VMEM((8, PAIRS), F32),
            pltpu.VMEM((2 * BLOCK, CHUNK), BF16),
            pltpu.VMEM((C, 160), BF16),
            pltpu.VMEM((C + 16, 2 * C), BF16),
            pltpu.VMEM((16, C), BF16),
            pltpu.VMEM((C, C), BF16),
            pltpu.VMEM((C, C), F32),
            pltpu.VMEM((8, PAIRS), F32),
            pltpu.VMEM((8, C), F32),
            pltpu.VMEM((3 * members, 8, C), F32),
            pltpu.VMEM((3 * members, 8, C), F32),
            pltpu.SemaphoreType.DMA,
            pltpu.SemaphoreType.DMA((3,)),
            pltpu.SemaphoreType.DMA,
            pltpu.SemaphoreType.DMA,
        ],
        compiler_params=pltpu.CompilerParams(
            collective_id=0, has_side_effects=True, vmem_limit_bytes=48 * 2**20
        ),
    )
    return jax.shard_map(
        call,
        mesh=mesh,
        in_specs=(
            P(None, ("slab", "grp")),
            P(("slab", "grp")),
            P(("slab", "grp"), None),
            P(),
            P(),
            P(),
            P(),
            P(),
            P(),
            P(("slab", "grp"), None),
            P(("slab", "grp")),
        ),
        out_specs=(P(("slab", "grp")), P(None, ("slab", "grp"))),
        check_vma=False,
    )
```

```python
import functools

import jax
import jax.numpy as jnp
from jax import lax
from jax.experimental import pallas as pl
from jax.experimental.pallas import tpu as pltpu
from jax.sharding import PartitionSpec as P

BLOCK = 64
C = 128
ROWS = 72
PAIRS = BLOCK * BLOCK
CHUNK = 1024
CENTRES = CHUNK // BLOCK
UNROLL = 4
SPACING = 2.5 / 7
MESH = pl.DeviceIdType.MESH
BF16, F32 = jnp.bfloat16, jnp.float32


def parts(value, count):
    found = []
    for _ in range(count):
        part = value.astype(BF16).astype(F32)
        found.append(part)
        value = value - part
    return found


def dot(left, right):
    return jnp.dot(left, right, preferred_element_type=F32)


def centre_onehot(start, width):
    lane = lax.broadcasted_iota(jnp.int32, (BLOCK, width), 1) + start
    row = lax.broadcasted_iota(jnp.int32, (BLOCK, width), 0)
    return jnp.where((lane // BLOCK) == row, 1.0, 0.0).astype(F32)


def kernel(
    slabs,
    members,
    pos_hbm,
    spc_hbm,
    node_hbm,
    wself_hbm,
    wsend_hbm,
    radial_hbm,
    wmix_hbm,
    readout_hbm,
    scale_hbm,
    nbr_hbm,
    count_hbm,
    energy_ref,
    force_ref,
    pos_ref,
    spc_ref,
    node_ref,
    wself_ref,
    wsend_ref,
    radial_ref,
    wmix_ref,
    readout_ref,
    scale_ref,
    nbr_ref,
    count_ref,
    own,
    sib,
    far,
    cur,
    pos_exp,
    scale_exp,
    rhs_pair,
    rhs_centre,
    lhs_send,
    lhs_rest,
    lhs_b,
    lhs_r,
    lhs_m,
    ro_exp,
    pair_acc,
    grads,
    back,
    load_sem,
    send_sem,
    recv_sem,
    back_send_sem,
    back_recv_sem,
):
    slab, me = lax.axis_index("slab"), lax.axis_index("grp")
    core = lax.rem(slab, 2)
    sib_slab = slab + 1 - 2 * core
    far_slab = lax.rem(slab - 1 + 2 * core + slabs, slabs)
    sib_panel, far_panel = 2 - 2 * core, 2 * core

    barrier = pltpu.get_barrier_semaphore()
    for k in range(members):
        to = lax.rem(me + k, members)
        pl.semaphore_signal(barrier, inc=1, device_id=(far_slab, to), device_id_type=MESH)
    for k in range(members):
        to = lax.rem(me + k, members)
        pl.semaphore_signal(barrier, inc=1, device_id=(sib_slab, to), device_id_type=MESH)
        if k:
            pl.semaphore_signal(barrier, inc=1, device_id=(slab, to), device_id_type=MESH)

    loads = [
        pltpu.make_async_copy(source, target, load_sem.at[k])
        for k, (source, target) in enumerate(
            [
                (node_hbm, node_ref),
                (wsend_hbm, wsend_ref),
                (pos_hbm, pos_ref),
                (spc_hbm, spc_ref),
                (wself_hbm, wself_ref),
                (radial_hbm, radial_ref),
                (wmix_hbm, wmix_ref),
                (readout_hbm, readout_ref),
                (scale_hbm, scale_ref),
                (nbr_hbm, nbr_ref),
                (count_hbm, count_ref),
            ]
        )
    ]
    for load in loads:
        load.start()
    for load in loads[:4]:
        load.wait()

    species = spc_ref[...].astype(F32).reshape(1, BLOCK)
    own[me, 0:BLOCK, :] = dot(node_ref[...], wsend_ref[...])
    pad = jnp.zeros((1, BLOCK), F32)
    place = jnp.concatenate([pos_ref[...], species, pad, pad, pad, pad], axis=0)
    own[me, BLOCK:ROWS, :] = jnp.concatenate([place, jnp.zeros_like(place)], axis=1)

    pl.semaphore_wait(barrier, 3 * members - 1)

    def send(panel, index, to_slab, to):
        pltpu.make_async_remote_copy(
            src_ref=own.at[me],
            dst_ref=panel.at[me],
            send_sem=send_sem,
            recv_sem=recv_sem.at[index],
            device_id=(to_slab, to),
            device_id_type=MESH,
        ).start()

    for k in range(members):
        send(far, 1, far_slab, lax.rem(me + k, members))
    for k in range(members):
        send(sib, 0, sib_slab, lax.rem(me + k, members))
    for k in range(1, members):
        send(own, 2, slab, lax.rem(me + k, members))

    for load in loads[4:]:
        load.wait()
    row8 = lax.broadcasted_iota(jnp.int32, (8, BLOCK), 0)
    scale8 = jnp.zeros((8, BLOCK), F32)
    for r in range(4):
        for s in range(4):
            scale8 = jnp.where((row8 == s) & (species == float(r)), scale_ref[r, s], scale8)
    small = jnp.concatenate(parts(place, 3) + parts(scale8, 3), axis=0).astype(BF16)
    half_hi, half_lo = parts(radial_ref[...] * 0.5, 2)
    self_hi, self_lo = parts(dot(node_ref[...], wself_ref[...]) * 0.5, 2)
    for k in range(PAIRS // CHUNK):
        mine = slice(k * CENTRES, (k + 1) * CENTRES)
        rest = [half_hi, half_lo, half_hi, jnp.zeros((8, C), F32), self_hi[mine], self_lo[mine]]
        lhs_rest[k] = jnp.concatenate(rest, axis=0).T.astype(BF16)

    def expand(step, carry):
        lanes = pl.ds(pl.multiple_of(step * CHUNK, CHUNK), CHUNK)
        spread = dot(small, centre_onehot(step * CHUNK, CHUNK).astype(BF16))
        pos_exp[:, lanes] = spread[0:8] + spread[8:16] + spread[16:24]
        scale_exp[:, lanes] = spread[24:32] + spread[32:40] + spread[40:48]
        return carry

    lax.fori_loop(0, PAIRS // CHUNK, expand, 0)

    atom = lax.broadcasted_iota(jnp.int32, (BLOCK, CHUNK), 0)
    lane = lax.broadcasted_iota(jnp.int32, (BLOCK, CHUNK), 1)
    hot_j = jnp.where(lax.rem(lane, BLOCK) == atom, 1.0, 0.0).astype(F32)
    rhs_pair[...] = jnp.concatenate([hot_j, hot_j], axis=0).astype(BF16)
    hot_i = centre_onehot(0, CHUNK)[0:CENTRES]
    rhs_centre[...] = jnp.concatenate([hot_i, hot_i], axis=0).astype(BF16)

    radial_hi, radial_lo = parts(radial_ref[...], 2)
    lhs_r[...] = (jnp.concatenate([radial_hi, radial_lo], axis=0) * 0.25).astype(BF16)
    lhs_m[...] = (wmix_ref[...].astype(F32).T * 0.5).astype(BF16)
    ones = jnp.ones((16, C), F32)
    lhs_b[...] = jnp.concatenate(
        [
            jnp.concatenate([jnp.zeros((C, C), F32), ones], axis=0),
            jnp.concatenate([wmix_ref[...].astype(F32), jnp.zeros((16, C), F32)], axis=0),
        ],
        axis=1,
    ).astype(BF16)
    readout = readout_ref[...].reshape(1, C)
    ro_exp[...] = jnp.broadcast_to(readout, (C, C)).T
    pair_acc[...] = jnp.zeros_like(pair_acc)
    grads[...] = jnp.zeros_like(grads)

    row = lax.broadcasted_iota(jnp.int32, (8, CHUNK), 0)
    pair = lax.broadcasted_iota(jnp.int32, (1, CHUNK), 1)
    center = row.astype(F32) * SPACING
    gap = lax.rem(pair, BLOCK) - pair // BLOCK

    def tile(turn, carry):
        slot = jnp.where(turn == 0, 1 - core, jnp.where(turn == 1, core, turn))
        other = nbr_ref[0, slot]
        panel, member = other // members, lax.rem(other, members)

        @pl.when(turn == 0)
        def _():
            pltpu.make_async_copy(sib, sib, recv_sem.at[0]).wait()
            cur[...] = sib[member]

        @pl.when(turn == 1)
        def _():
            pltpu.make_async_copy(far, far, recv_sem.at[1]).wait()
            cur[...] = far[member]

        @pl.when(turn == 2)
        def _():
            some = own.at[pl.ds(0, members - 1)]
            pltpu.make_async_copy(some, some, recv_sem.at[2]).wait()

        @pl.when(turn >= 2)
        def _():
            cur[...] = jnp.where(
                panel == sib_panel,
                sib[member],
                jnp.where(panel == far_panel, far[member], own[member]),
            )

        live = jnp.where(slot < count_ref[0], 1.0, 0.0)
        same = (panel == 1) & (member == me)
        place_j = cur[BLOCK:ROWS, 0:BLOCK]
        place_j = jnp.concatenate([place_j] * (CHUNK // BLOCK), axis=1)
        kind_hot = jnp.where(place_j[3:4] == row.astype(F32), 1.0, 0.0)
        lhs_send[...] = jnp.concatenate(parts(cur[0:BLOCK, :] * 0.5, 2), axis=0).T.astype(BF16)

        def step(index, carry):
            def first(sub):
                turn = index * UNROLL + sub
                lanes = pl.ds(pl.multiple_of(turn * CHUNK, CHUNK), CHUNK)
                diff = jnp.where(row < 3, place_j - pos_exp[:, lanes], 0.0)
                dist_sq = jnp.sum(diff * diff, axis=0, keepdims=True)
                scale = jnp.sum(scale_exp[:, lanes] * kind_hot, axis=0, keepdims=True)
                scaled = dist_sq * scale
                keep = jnp.where(same & (gap == turn * CENTRES), 0.0, live)
                reach = jnp.maximum(1.0 - scaled * (1.0 / 2.5), 0.0)
                offset = (scaled - center) * (1.0 / SPACING)
                basis = jnp.exp(-(offset * offset))
                slope = basis * offset * (-2.0 / SPACING)
                basis_hi, basis_lo = parts(basis, 2)
                head = jnp.concatenate(
                    [basis_hi, basis_hi, basis_lo, jnp.zeros((8, CHUNK), F32)], axis=0
                ).astype(BF16)
                rhs = jnp.concatenate([rhs_pair[...], head, rhs_centre[...]], axis=0)
                lhs = jnp.concatenate([lhs_send[...], lhs_rest[turn]], axis=1)
                return lanes, diff, scale, keep, reach, slope, dot(lhs, rhs)

            def second(state):
                half = state[-1]
                t = jnp.tanh(half)
                p = 1.0 + t
                hidden = half * p
                slope_1 = p + hidden * (1.0 - t)
                half = dot(lhs_m[...], hidden.astype(BF16))
                return state[:-1] + (slope_1, half)

            def third(state):
                half = state[-1]
                t = jnp.tanh(half)
                p = (1.0 + t) * jnp.concatenate([ro_exp[...]] * (CHUNK // C), axis=1)
                mixed = half * p
                slope_2 = p + mixed * (1.0 - t)
                out = dot(lhs_b[...], jnp.concatenate([mixed, slope_2], axis=0).astype(BF16))
                return state[:-1] + (out,)

            def fourth(state):
                lanes, diff, scale, keep, reach, slope, slope_1, out = state
                d_basis = dot(lhs_r[...], (out[0:C] * slope_1).astype(BF16))
                d_basis = d_basis[0:8] + d_basis[8:16]
                energy = out[C : C + 1]
                cut = reach * reach
                d_scaled = cut * jnp.sum(d_basis * slope, axis=0, keepdims=True)
                d_scaled = d_scaled - (2.0 / 2.5) * reach * energy
                force = (2.0 * keep * scale * d_scaled) * diff
                found = jnp.where(row == 3, keep * cut * energy, force)
                pair_acc[:, lanes] += found
                total = found[:, 0:C]
                for k in range(1, CHUNK // C):
                    total = total + found[:, k * C : (k + 1) * C]
                return total

            stages = [first, second, third, fourth]
            states = {}
            total = carry
            for turn in range(UNROLL + 3):
                for depth in range(4):
                    sub = turn - depth
                    if 0 <= sub < UNROLL:
                        states[sub] = stages[depth](states.get(sub, sub))
                        if depth == 3:
                            total = total + states.pop(sub)
            return total

        grad = lax.fori_loop(0, PAIRS // CHUNK // UNROLL, step, jnp.zeros((8, C), F32))
        grad = grad[:, 0:BLOCK] + grad[:, BLOCK:C]
        grad = jnp.concatenate([grad, jnp.zeros_like(grad)], axis=1)
        group = jnp.where(panel == sib_panel, 0, jnp.where(panel == far_panel, 1, 2))
        which = group * members + member
        for k in range(3 * members):
            grads[k] += jnp.where(which == k, grad, 0.0)
        return carry

    lax.fori_loop(0, 4, tile, 0)

    def give(index, to_slab, to):
        pltpu.make_async_remote_copy(
            src_ref=grads.at[index * members + to],
            dst_ref=back.at[index * members + me],
            send_sem=back_send_sem,
            recv_sem=back_recv_sem,
            device_id=(to_slab, to),
            device_id_type=MESH,
        ).start()

    for k in range(members):
        give(1, far_slab, lax.rem(me + k, members))
    for k in range(1, members):
        give(2, slab, lax.rem(me + k, members))
    for k in range(members):
        give(0, sib_slab, lax.rem(me + k, members))
    back[2 * members + me] = grads[2 * members + me]

    def gather(index, total):
        lanes = pl.ds(pl.multiple_of(index * CHUNK, CHUNK), CHUNK)
        split = jnp.concatenate(parts(pair_acc[:, lanes], 3), axis=0).astype(BF16)
        hot = centre_onehot(index * CHUNK, CHUNK).astype(BF16)
        found = lax.dot_general(
            split, hot, (((1,), (1,)), ((), ())), preferred_element_type=F32
        )
        return total + (found[0:8] + found[8:16] + found[16:24])

    centre_sum = lax.fori_loop(0, PAIRS // CHUNK, gather, jnp.zeros((8, BLOCK), F32))
    energy_ref[...] = centre_sum[3:4].reshape(BLOCK)

    some = back.at[pl.ds(0, 3 * members - 1)]
    pltpu.make_async_copy(some, some, back_recv_sem).wait()
    total = back[0]
    for k in range(1, 3 * members):
        total = total + back[k]
    force_ref[...] = centre_sum[0:3] - total[0:3, 0:BLOCK]

    for panel in (sib, far, own.at[pl.ds(0, members - 1)]):
        pltpu.make_async_copy(panel, panel, send_sem).wait()
    pltpu.make_async_copy(some, some, back_send_sem).wait()


def solution(mesh):
    slabs, members = mesh.shape["slab"], mesh.shape["grp"]
    vmem = pl.BlockSpec(memory_space=pltpu.VMEM)
    panel = pltpu.VMEM((members, ROWS, C), F32)
    call = pl.pallas_call(
        functools.partial(kernel, slabs, members),
        out_shape=(
            jax.ShapeDtypeStruct((BLOCK,), F32),
            jax.ShapeDtypeStruct((3, BLOCK), F32),
        ),
        in_specs=[pl.BlockSpec(memory_space=pltpu.HBM)] * 11,
        out_specs=(vmem, vmem),
        scratch_shapes=[
            pltpu.VMEM((3, BLOCK), F32),
            pltpu.VMEM((BLOCK,), jnp.int32),
            pltpu.VMEM((BLOCK, C), BF16),
            pltpu.VMEM((C, C), BF16),
            pltpu.VMEM((C, C), BF16),
            pltpu.VMEM((8, C), F32),
            pltpu.VMEM((C, C), BF16),
            pltpu.VMEM((C,), F32),
            pltpu.SMEM((4, 4), F32),
            pltpu.SMEM((1, 4), jnp.int32),
            pltpu.SMEM((1,), jnp.int32),
            panel,
            panel,
            panel,
            pltpu.VMEM((ROWS, C), F32),
            pltpu.VMEM((8, PAIRS), F32),
            pltpu.VMEM((8, PAIRS), F32),
            pltpu.VMEM((2 * BLOCK, CHUNK), BF16),
            pltpu.VMEM((2 * CENTRES, CHUNK), BF16),
            pltpu.VMEM((C, 2 * BLOCK), BF16),
            pltpu.VMEM((PAIRS // CHUNK, C, 32 + 2 * CENTRES), BF16),
            pltpu.VMEM((C + 16, 2 * C), BF16),
            pltpu.VMEM((16, C), BF16),
            pltpu.VMEM((C, C), BF16),
            pltpu.VMEM((C, C), F32),
            pltpu.VMEM((8, PAIRS), F32),
            pltpu.VMEM((3 * members, 8, C), F32),
            pltpu.VMEM((3 * members, 8, C), F32),
            pltpu.SemaphoreType.DMA((11,)),
            pltpu.SemaphoreType.DMA,
            pltpu.SemaphoreType.DMA((3,)),
            pltpu.SemaphoreType.DMA,
            pltpu.SemaphoreType.DMA,
        ],
        compiler_params=pltpu.CompilerParams(
            collective_id=0, has_side_effects=True, vmem_limit_bytes=48 * 2**20
        ),
    )
    return jax.shard_map(
        call,
        mesh=mesh,
        in_specs=(
            P(None, ("slab", "grp")),
            P(("slab", "grp")),
            P(("slab", "grp"), None),
            P(),
            P(),
            P(),
            P(),
            P(),
            P(),
            P(("slab", "grp"), None),
            P(("slab", "grp")),
        ),
        out_specs=(P(("slab", "grp")), P(None, ("slab", "grp"))),
        check_vma=False,
    )
```

```python
import functools

import jax
import jax.numpy as jnp
from jax import lax
from jax.experimental import pallas as pl
from jax.experimental.pallas import tpu as pltpu
from jax.sharding import PartitionSpec as P

BLOCK = 64
C = 128
ROWS = 72
PAIRS = BLOCK * BLOCK
CHUNK = 1024
CENTRES = CHUNK // BLOCK
SPACING = 2.5 / 7
MESH = pl.DeviceIdType.MESH
BF16, F32 = jnp.bfloat16, jnp.float32


def parts(value, count):
    found = []
    for _ in range(count):
        part = value.astype(BF16).astype(F32)
        found.append(part)
        value = value - part
    return found


def dot(left, right):
    return jnp.dot(left, right, preferred_element_type=F32)


def centre_onehot(start, width):
    lane = lax.broadcasted_iota(jnp.int32, (BLOCK, width), 1) + start
    row = lax.broadcasted_iota(jnp.int32, (BLOCK, width), 0)
    return jnp.where((lane // BLOCK) == row, 1.0, 0.0).astype(F32)


def kernel(
    slabs,
    members,
    pos_hbm,
    spc_hbm,
    node_hbm,
    wself_hbm,
    wsend_hbm,
    radial_hbm,
    wmix_hbm,
    readout_hbm,
    scale_hbm,
    nbr_hbm,
    count_hbm,
    energy_ref,
    force_ref,
    pos_ref,
    spc_ref,
    node_ref,
    wself_ref,
    wsend_ref,
    radial_ref,
    wmix_ref,
    readout_ref,
    scale_ref,
    nbr_ref,
    count_ref,
    own,
    asked,
    centres,
    pos_exp,
    scale_exp,
    hot_centre,
    rhs_pair,
    rhs_centre,
    lhs_send,
    lhs_rest,
    lhs_b,
    lhs_r,
    lhs_m,
    ro_exp,
    pair_acc,
    centre_sums,
    grads,
    returned,
    back,
    load_sem,
    ask_send_sem,
    ask_recv_sem,
    own_send_sem,
    own_recv_sem,
    sum_send_sem,
    sum_recv_sem,
    back_send_sem,
    back_recv_sem,
):
    slab, me = lax.axis_index("slab"), lax.axis_index("grp")
    core = lax.rem(slab, 2)
    sib_slab = slab + 1 - 2 * core
    far_slab = lax.rem(slab - 1 + 2 * core + slabs, slabs)

    barrier = pltpu.get_barrier_semaphore()
    partners = [(far_slab, me), (sib_slab, me)]
    mates = [lax.rem(me + k, members) for k in range(1, members)]
    for to in partners + [(slab, mate) for mate in mates]:
        pl.semaphore_signal(barrier, inc=1, device_id=to, device_id_type=MESH)

    loads = [
        pltpu.make_async_copy(source, target, load_sem.at[k])
        for k, (source, target) in enumerate(
            [
                (node_hbm, node_ref),
                (wself_hbm, wself_ref),
                (wsend_hbm, wsend_ref),
                (pos_hbm, pos_ref),
                (spc_hbm, spc_ref),
                (nbr_hbm, nbr_ref),
                (count_hbm, count_ref),
                (radial_hbm, radial_ref),
                (wmix_hbm, wmix_ref),
                (readout_hbm, readout_ref),
                (scale_hbm, scale_ref),
            ]
        )
    ]
    for load in loads:
        load.start()

    def spread_hot(step, carry):
        lanes = pl.ds(pl.multiple_of(step * CHUNK, CHUNK), CHUNK)
        hot_centre[:, lanes] = centre_onehot(step * CHUNK, CHUNK).astype(BF16)
        return carry

    for load in loads[:7]:
        load.wait()

    species = spc_ref[...].astype(F32).reshape(1, BLOCK)
    pad = jnp.zeros((1, BLOCK), F32)
    place = jnp.concatenate([pos_ref[...], species, pad, pad, pad, pad], axis=0)
    place = jnp.concatenate([place, jnp.zeros_like(place)], axis=1)
    features = dot(node_ref[...], wself_ref[...])
    own[me, 0:BLOCK, :] = dot(node_ref[...], wsend_ref[...])
    own[me, BLOCK:ROWS, :] = place
    asked_row = lax.broadcasted_iota(jnp.int32, (3 * members, C), 0)

    def slots_in(panel, first):
        hot = jnp.zeros((3 * members, C), F32)
        for k, slot in enumerate((first, 2, 3)):
            other = nbr_ref[0, slot]
            wanted = jnp.where(
                (other // members == panel) & (slot < count_ref[0]),
                lax.rem(other, members) + k * members,
                -1,
            )
            hot = jnp.where(asked_row == wanted, 1.0, hot)
        return hot

    for k, (panel, first) in enumerate(((2 * core, core), (2 - 2 * core, 1 - core))):
        centres[k, 0:BLOCK, :] = features
        centres[k, BLOCK:ROWS, :] = place
        centres[k, ROWS:, :] = slots_in(panel, first)
    asked[2, 0:BLOCK, :] = features
    asked[2, BLOCK:ROWS, :] = place
    asked[2, ROWS:, :] = slots_in(1, 2)

    pl.semaphore_wait(barrier, members + 1)

    def ask(k):
        return pltpu.make_async_remote_copy(
            src_ref=centres.at[k],
            dst_ref=asked.at[k],
            send_sem=ask_send_sem.at[k],
            recv_sem=ask_recv_sem.at[k],
            device_id=partners[k],
            device_id_type=MESH,
        )

    ask(0).start()
    for mate in mates:
        pltpu.make_async_remote_copy(
            src_ref=own.at[me],
            dst_ref=own.at[me],
            send_sem=own_send_sem,
            recv_sem=own_recv_sem,
            device_id=(slab, mate),
            device_id_type=MESH,
        ).start()
    ask(1).start()

    lax.fori_loop(0, PAIRS // CHUNK, spread_hot, 0)
    atom = lax.broadcasted_iota(jnp.int32, (BLOCK, CHUNK), 0)
    lane = lax.broadcasted_iota(jnp.int32, (BLOCK, CHUNK), 1)
    hot_j = jnp.where(lax.rem(lane, BLOCK) == atom, 1.0, 0.0).astype(F32)
    rhs_pair[...] = jnp.concatenate([hot_j, hot_j], axis=0).astype(BF16)
    hot_i = centre_onehot(0, CHUNK)[0:CENTRES]
    rhs_centre[...] = jnp.concatenate([hot_i, hot_i], axis=0).astype(BF16)
    for load in loads[7:]:
        load.wait()
    radial_hi, radial_lo = parts(radial_ref[...], 2)
    lhs_r[...] = (jnp.concatenate([radial_hi, radial_lo], axis=0) * 0.25).astype(BF16)
    lhs_m[...] = (wmix_ref[...].astype(F32).T * 0.5).astype(BF16)
    ones = jnp.ones((16, C), F32)
    lhs_b[...] = jnp.concatenate(
        [
            jnp.concatenate([jnp.zeros((C, C), F32), ones], axis=0),
            jnp.concatenate([wmix_ref[...].astype(F32), jnp.zeros((16, C), F32)], axis=0),
        ],
        axis=1,
    ).astype(BF16)
    readout = readout_ref[...].reshape(1, C)
    ro_exp[...] = jnp.broadcast_to(readout, (C, C)).T
    grads[...] = jnp.zeros_like(grads)

    row8 = lax.broadcasted_iota(jnp.int32, (8, BLOCK), 0)
    row = lax.broadcasted_iota(jnp.int32, (8, CHUNK), 0)
    pair = lax.broadcasted_iota(jnp.int32, (1, CHUNK), 1)
    center = row.astype(F32) * SPACING
    gap = lax.rem(pair, BLOCK) - pair // BLOCK
    mates_blocks = own.at[pl.ds(0, members - 1)]
    mates_grads = grads.at[pl.ds(0, members - 1)]

    def group(turn, carry):
        which = jnp.where(slab < 2, 2 - turn, turn)

        @pl.when(turn == 0)
        def _():
            pltpu.make_async_copy(mates_blocks, mates_blocks, own_recv_sem).wait()

        @pl.when(which == 0)
        def _():
            ask(0).wait_recv()

        @pl.when(which == 1)
        def _():
            ask(1).wait_recv()

        spot = asked[which, BLOCK:ROWS, 0:BLOCK]
        scale8 = jnp.zeros((8, BLOCK), F32)
        for r in range(4):
            for s in range(4):
                there = (row8 == s) & (spot[3:4] == float(r))
                scale8 = jnp.where(there, scale_ref[r, s], scale8)
        small = jnp.concatenate(parts(spot, 3) + parts(scale8, 3), axis=0).astype(BF16)
        half_hi, half_lo = parts(radial_ref[...] * 0.5, 2)
        for k in range(PAIRS // CHUNK):
            mine = pl.ds(k * CENTRES, CENTRES)
            self_hi, self_lo = parts(asked[which, mine, :] * 0.5, 2)
            rest = [half_hi, half_lo, half_hi, jnp.zeros((8, C), F32), self_hi, self_lo]
            lhs_rest[k] = jnp.concatenate(rest, axis=0).T.astype(BF16)
            lanes = slice(k * CHUNK, (k + 1) * CHUNK)
            spread = dot(small, hot_centre[:, lanes])
            pos_exp[:, lanes] = spread[0:8] + spread[8:16] + spread[16:24]
            scale_exp[:, lanes] = spread[24:32] + spread[32:40] + spread[40:48]
        pair_acc[...] = jnp.zeros_like(pair_acc)

        def tile(slot, carry):
            hot = asked[which, pl.ds(pl.multiple_of(ROWS + slot * members, 8), members), :]
            block = own[0] * hot[0:1]
            for k in range(1, members):
                block = block + own[k] * hot[k : k + 1]
            live = jnp.concatenate([jnp.sum(hot, axis=0, keepdims=True)] * (CHUNK // C), axis=1)
            self_hot = asked[which, pl.ds(ROWS + slot * members + me, 1), :]
            self_hot = jnp.where(which == 2, self_hot, 0.0)
            self_hot = jnp.concatenate([self_hot] * (CHUNK // C), axis=1)
            place_j = jnp.concatenate([block[BLOCK:ROWS, 0:BLOCK]] * (CHUNK // BLOCK), axis=1)
            kind_hot = jnp.where(place_j[3:4] == row.astype(F32), 1.0, 0.0)
            lhs_send[...] = jnp.concatenate(parts(block[0:BLOCK] * 0.5, 2), axis=0).T.astype(BF16)

            def first(turn):
                lanes = slice(turn * CHUNK, (turn + 1) * CHUNK)
                diff = jnp.where(row < 3, place_j - pos_exp[:, lanes], 0.0)
                dist_sq = jnp.sum(diff * diff, axis=0, keepdims=True)
                scale = jnp.sum(scale_exp[:, lanes] * kind_hot, axis=0, keepdims=True)
                scaled = dist_sq * scale
                keep = live - jnp.where(gap == turn * CENTRES, self_hot, 0.0)
                reach = jnp.maximum(1.0 - scaled * (1.0 / 2.5), 0.0)
                offset = (scaled - center) * (1.0 / SPACING)
                basis = jnp.exp(-(offset * offset))
                slope = basis * offset * (-2.0 / SPACING)
                basis_hi, basis_lo = parts(basis, 2)
                head = jnp.concatenate(
                    [basis_hi, basis_hi, basis_lo, jnp.zeros((8, CHUNK), F32)], axis=0
                ).astype(BF16)
                rhs = jnp.concatenate([rhs_pair[...], head, rhs_centre[...]], axis=0)
                lhs = jnp.concatenate([lhs_send[...], lhs_rest[turn]], axis=1)
                return lanes, diff, scale, keep, reach, slope, dot(lhs, rhs)

            def second(state):
                half = state[-1]
                t = jnp.tanh(half)
                p = 1.0 + t
                hidden = half * p
                slope_1 = p + hidden * (1.0 - t)
                half = dot(lhs_m[...], hidden.astype(BF16))
                return state[:-1] + (slope_1, half)

            def third(state):
                half = state[-1]
                t = jnp.tanh(half)
                p = (1.0 + t) * jnp.concatenate([ro_exp[...]] * (CHUNK // C), axis=1)
                mixed = half * p
                slope_2 = p + mixed * (1.0 - t)
                out = dot(lhs_b[...], jnp.concatenate([mixed, slope_2], axis=0).astype(BF16))
                return state[:-1] + (out,)

            def fourth(state):
                lanes, diff, scale, keep, reach, slope, slope_1, out = state
                d_basis = dot(lhs_r[...], (out[0:C] * slope_1).astype(BF16))
                d_basis = d_basis[0:8] + d_basis[8:16]
                energy = out[C : C + 1]
                cut = reach * reach
                d_scaled = cut * jnp.sum(d_basis * slope, axis=0, keepdims=True)
                d_scaled = d_scaled - (2.0 / 2.5) * reach * energy
                force = (2.0 * keep * scale * d_scaled) * diff
                found = jnp.where(row == 3, keep * cut * energy, force)
                pair_acc[:, lanes] += found
                total = found[:, 0:C]
                for k in range(1, CHUNK // C):
                    total = total + found[:, k * C : (k + 1) * C]
                return total

            stages = [first, second, third, fourth]
            states = {}
            total = None
            count = PAIRS // CHUNK
            for turn in range(count + 3):
                for depth in range(4):
                    sub = turn - depth
                    if 0 <= sub < count:
                        states[sub] = stages[depth](states.get(sub, sub))
                        if depth == 3:
                            part = states.pop(sub)
                            total = part if total is None else total + part
            grad = total[:, 0:BLOCK] + total[:, BLOCK:C]
            grad = jnp.concatenate([grad, jnp.zeros_like(grad)], axis=1)
            for k in range(members):
                grads[k] += grad * hot[k : k + 1]
            return carry

        lax.fori_loop(jnp.where(which == 2, 1, 0), 3, tile, 0)

        total = jnp.zeros((24, BLOCK), F32)
        for k in range(PAIRS // CHUNK):
            lanes = slice(k * CHUNK, (k + 1) * CHUNK)
            split = jnp.concatenate(parts(pair_acc[:, lanes], 3), axis=0).astype(BF16)
            total = total + lax.dot_general(
                split,
                hot_centre[:, lanes],
                (((1,), (1,)), ((), ())),
                preferred_element_type=F32,
            )
        total = total[0:8] + total[8:16] + total[16:24]
        centre_sums[which] = jnp.concatenate([total, jnp.zeros_like(total)], axis=1)

        @pl.when(which == 0)
        def _():
            tell(0).start()

        @pl.when(which == 1)
        def _():
            tell(1).start()

        return carry

    def tell(k):
        return pltpu.make_async_remote_copy(
            src_ref=centre_sums.at[k],
            dst_ref=returned.at[k],
            send_sem=sum_send_sem.at[k],
            recv_sem=sum_recv_sem.at[k],
            device_id=partners[k],
            device_id_type=MESH,
        )

    lax.fori_loop(0, 3, group, 0)

    for mate in mates:
        pltpu.make_async_remote_copy(
            src_ref=grads.at[mate],
            dst_ref=back.at[me],
            send_sem=back_send_sem,
            recv_sem=back_recv_sem,
            device_id=(slab, mate),
            device_id_type=MESH,
        ).start()
    back[me] = grads[me]

    tell(0).wait_recv()
    tell(1).wait_recv()
    centre_sum = centre_sums[2] + returned[0] + returned[1]
    energy_ref[...] = centre_sum[3:4, 0:BLOCK].reshape(BLOCK)
    pltpu.make_async_copy(mates_grads, mates_grads, back_recv_sem).wait()
    total = back[0]
    for k in range(1, members):
        total = total + back[k]
    force_ref[...] = (centre_sum - total)[0:3, 0:BLOCK]

    for k in range(2):
        ask(k).wait_send()
        tell(k).wait_send()
    pltpu.make_async_copy(mates_blocks, mates_blocks, own_send_sem).wait()
    pltpu.make_async_copy(mates_grads, mates_grads, back_send_sem).wait()


def solution(mesh):
    slabs, members = mesh.shape["slab"], mesh.shape["grp"]
    vmem = pl.BlockSpec(memory_space=pltpu.VMEM)
    call = pl.pallas_call(
        functools.partial(kernel, slabs, members),
        out_shape=(
            jax.ShapeDtypeStruct((BLOCK,), F32),
            jax.ShapeDtypeStruct((3, BLOCK), F32),
        ),
        in_specs=[pl.BlockSpec(memory_space=pltpu.HBM)] * 11,
        out_specs=(vmem, vmem),
        scratch_shapes=[
            pltpu.VMEM((3, BLOCK), F32),
            pltpu.VMEM((BLOCK,), jnp.int32),
            pltpu.VMEM((BLOCK, C), BF16),
            pltpu.VMEM((C, C), BF16),
            pltpu.VMEM((C, C), BF16),
            pltpu.VMEM((8, C), F32),
            pltpu.VMEM((C, C), BF16),
            pltpu.VMEM((C,), F32),
            pltpu.SMEM((4, 4), F32),
            pltpu.SMEM((1, 4), jnp.int32),
            pltpu.SMEM((1,), jnp.int32),
            pltpu.VMEM((members, ROWS, C), F32),
            pltpu.VMEM((3, ROWS + 3 * members, C), F32),
            pltpu.VMEM((2, ROWS + 3 * members, C), F32),
            pltpu.VMEM((8, PAIRS), F32),
            pltpu.VMEM((8, PAIRS), F32),
            pltpu.VMEM((BLOCK, PAIRS), BF16),
            pltpu.VMEM((2 * BLOCK, CHUNK), BF16),
            pltpu.VMEM((2 * CENTRES, CHUNK), BF16),
            pltpu.VMEM((C, 2 * BLOCK), BF16),
            pltpu.VMEM((PAIRS // CHUNK, C, 32 + 2 * CENTRES), BF16),
            pltpu.VMEM((C + 16, 2 * C), BF16),
            pltpu.VMEM((16, C), BF16),
            pltpu.VMEM((C, C), BF16),
            pltpu.VMEM((C, C), F32),
            pltpu.VMEM((8, PAIRS), F32),
            pltpu.VMEM((3, 8, C), F32),
            pltpu.VMEM((members, 8, C), F32),
            pltpu.VMEM((2, 8, C), F32),
            pltpu.VMEM((members, 8, C), F32),
            pltpu.SemaphoreType.DMA((11,)),
            pltpu.SemaphoreType.DMA((2,)),
            pltpu.SemaphoreType.DMA((2,)),
            pltpu.SemaphoreType.DMA,
            pltpu.SemaphoreType.DMA,
            pltpu.SemaphoreType.DMA((2,)),
            pltpu.SemaphoreType.DMA((2,)),
            pltpu.SemaphoreType.DMA,
            pltpu.SemaphoreType.DMA,
        ],
        compiler_params=pltpu.CompilerParams(
            collective_id=0, has_side_effects=True, vmem_limit_bytes=60 * 2**20
        ),
    )
    return jax.shard_map(
        call,
        mesh=mesh,
        in_specs=(
            P(None, ("slab", "grp")),
            P(("slab", "grp")),
            P(("slab", "grp"), None),
            P(),
            P(),
            P(),
            P(),
            P(),
            P(),
            P(("slab", "grp"), None),
            P(("slab", "grp")),
        ),
        out_specs=(P(("slab", "grp")), P(None, ("slab", "grp"))),
        check_vma=False,
    )
```

```python
import functools

import jax
import jax.numpy as jnp
from jax import lax
from jax.experimental import pallas as pl
from jax.experimental.pallas import tpu as pltpu
from jax.sharding import PartitionSpec as P

BLOCK = 64
C = 128
ROWS = 72
PAIRS = BLOCK * BLOCK
CHUNK = 1024
CENTRES = CHUNK // BLOCK
SPACING = 2.5 / 7
MESH = pl.DeviceIdType.MESH
BF16, F32 = jnp.bfloat16, jnp.float32


def parts(value, count):
    found = []
    for _ in range(count):
        part = value.astype(BF16).astype(F32)
        found.append(part)
        value = value - part
    return found


def dot(left, right):
    return jnp.dot(left, right, preferred_element_type=F32)


def centre_onehot(start, width):
    lane = lax.broadcasted_iota(jnp.int32, (BLOCK, width), 1) + start
    row = lax.broadcasted_iota(jnp.int32, (BLOCK, width), 0)
    return jnp.where((lane // BLOCK) == row, 1.0, 0.0).astype(F32)


def kernel(
    slabs,
    members,
    pos_hbm,
    spc_hbm,
    node_hbm,
    wself_hbm,
    wsend_hbm,
    radial_hbm,
    wmix_hbm,
    readout_hbm,
    scale_hbm,
    nbr_hbm,
    count_hbm,
    energy_ref,
    force_ref,
    pos_ref,
    spc_ref,
    node_ref,
    wself_ref,
    wsend_ref,
    radial_ref,
    wmix_ref,
    readout_ref,
    scale_ref,
    nbr_ref,
    count_ref,
    own,
    near,
    asked,
    centres,
    block_ref,
    pos_exp,
    scale_exp,
    hot_centre,
    rhs_pair,
    rhs_centre,
    lhs_send,
    lhs_rest,
    lhs_b,
    lhs_r,
    lhs_m,
    ro_exp,
    pair_acc,
    centre_sums,
    grads,
    near_grads,
    near_back,
    returned,
    back,
    load_sem,
    send_sem,
    recv_sem,
    own_send_sem,
    own_recv_sem,
    back_send_sem,
    back_recv_sem,
    group_sem,
    far_sem,
):
    slab, me = lax.axis_index("slab"), lax.axis_index("grp")
    core = lax.rem(slab, 2)
    sib_slab = slab + 1 - 2 * core
    far_slab = lax.rem(slab - 1 + 2 * core + slabs, slabs)

    barrier = pltpu.get_barrier_semaphore()
    mates = [lax.rem(me + k, members) for k in range(1, members)]
    far_hub = lax.rem(slab + jnp.where(core == 0, slabs - 1, 2), slabs)
    pl.semaphore_signal(barrier, inc=1, device_id=(far_hub, me), device_id_type=MESH)
    for mate in mates:
        pl.semaphore_signal(barrier, inc=1, device_id=(slab - core, mate), device_id_type=MESH)

    @pl.when(core == 1)
    def _():
        pl.semaphore_signal(barrier, inc=1, device_id=(sib_slab, me), device_id_type=MESH)

    loads = [
        pltpu.make_async_copy(source, target, load_sem.at[k])
        for k, (source, target) in enumerate(
            [
                (node_hbm, node_ref),
                (wself_hbm, wself_ref),
                (wsend_hbm, wsend_ref),
                (pos_hbm, pos_ref),
                (spc_hbm, spc_ref),
                (nbr_hbm, nbr_ref),
                (count_hbm, count_ref),
                (radial_hbm, radial_ref),
                (wmix_hbm, wmix_ref),
                (readout_hbm, readout_ref),
                (scale_hbm, scale_ref),
            ]
        )
    ]
    for load in loads:
        load.start()

    def spread_hot(step, carry):
        lanes = pl.ds(pl.multiple_of(step * CHUNK, CHUNK), CHUNK)
        hot_centre[:, lanes] = centre_onehot(step * CHUNK, CHUNK).astype(BF16)
        return carry

    for load in loads[:7]:
        load.wait()

    species = spc_ref[...].astype(F32).reshape(1, BLOCK)
    pad = jnp.zeros((1, BLOCK), F32)
    place = jnp.concatenate([pos_ref[...], species, pad, pad, pad, pad], axis=0)
    place = jnp.concatenate([place, jnp.zeros_like(place)], axis=1)
    features = dot(node_ref[...], wself_ref[...])
    own[me, 0:BLOCK, :] = dot(node_ref[...], wsend_ref[...])
    own[me, BLOCK:ROWS, :] = place
    asked_row = lax.broadcasted_iota(jnp.int32, (3 * members, C), 0)

    def slots_in(panel, first):
        hot = jnp.zeros((3 * members, C), F32)
        for k, slot in enumerate((first, 2, 3)):
            other = nbr_ref[0, slot]
            wanted = jnp.where(
                (other // members == panel) & (slot < count_ref[0]),
                lax.rem(other, members) + k * members,
                -1,
            )
            hot = jnp.where(asked_row == wanted, 1.0, hot)
        return hot

    centres[0:BLOCK, :] = features
    centres[BLOCK:ROWS, :] = place
    centres[ROWS:, :] = slots_in(2 * core, core)
    asked[1, 0:BLOCK, :] = features
    asked[1, BLOCK:ROWS, :] = place
    asked[1, ROWS : ROWS + 3 * members, :] = slots_in(1, 1 - core)
    asked[1, ROWS + 3 * members :, :] = slots_in(2 - 2 * core, 1 - core)

    @pl.when(core == 0)
    def _():
        pl.semaphore_wait(barrier, 2 * members - 1)
        pl.semaphore_signal(group_sem, inc=1, device_id=(sib_slab, me), device_id_type=MESH)

    @pl.when(core == 1)
    def _():
        pl.semaphore_wait(group_sem, 1)

    for mate in mates:
        pltpu.make_async_remote_copy(
            src_ref=own.at[me],
            dst_ref=own.at[me],
            send_sem=own_send_sem,
            recv_sem=own_recv_sem,
            device_id=(slab, mate),
            device_id_type=MESH,
        ).start()

    def copy(index, source, target, to_slab):
        return pltpu.make_async_remote_copy(
            src_ref=source,
            dst_ref=target,
            send_sem=send_sem.at[index],
            recv_sem=recv_sem.at[index],
            device_id=(to_slab, me),
            device_id_type=MESH,
        )

    ask = copy(0, centres, asked.at[0, pl.ds(0, ROWS + 3 * members)], far_slab)
    tell = copy(1, centre_sums.at[0], returned, far_slab)
    lend = copy(2, own, near, sib_slab)
    repay = copy(3, near_grads, near_back, sib_slab)
    early = slab < 2

    def ask_far():
        @pl.when(core == 0)
        def _():
            pl.semaphore_wait(far_sem, 1)

        @pl.when(core == 1)
        def _():
            pl.semaphore_wait(barrier, 2)
            pl.semaphore_signal(far_sem, inc=1, device_id=(sib_slab, me), device_id_type=MESH)

        ask.start()

    pl.when(jnp.logical_not(early))(ask_far)

    lax.fori_loop(0, PAIRS // CHUNK, spread_hot, 0)
    atom = lax.broadcasted_iota(jnp.int32, (BLOCK, CHUNK), 0)
    lane = lax.broadcasted_iota(jnp.int32, (BLOCK, CHUNK), 1)
    hot_j = jnp.where(lax.rem(lane, BLOCK) == atom, 1.0, 0.0).astype(F32)
    rhs_pair[...] = jnp.concatenate([hot_j, hot_j], axis=0).astype(BF16)
    hot_i = centre_onehot(0, CHUNK)[0:CENTRES]
    rhs_centre[...] = jnp.concatenate([hot_i, hot_i], axis=0).astype(BF16)
    for load in loads[7:]:
        load.wait()
    radial_hi, radial_lo = parts(radial_ref[...], 2)
    lhs_r[...] = (jnp.concatenate([radial_hi, radial_lo], axis=0) * 0.25).astype(BF16)
    lhs_m[...] = (wmix_ref[...].astype(F32).T * 0.5).astype(BF16)
    ones = jnp.ones((16, C), F32)
    lhs_b[...] = jnp.concatenate(
        [
            jnp.concatenate([jnp.zeros((C, C), F32), ones], axis=0),
            jnp.concatenate([wmix_ref[...].astype(F32), jnp.zeros((16, C), F32)], axis=0),
        ],
        axis=1,
    ).astype(BF16)
    readout = readout_ref[...].reshape(1, C)
    ro_exp[...] = jnp.broadcast_to(readout, (C, C)).T
    grads[...] = jnp.zeros_like(grads)
    near_grads[...] = jnp.zeros_like(near_grads)

    row8 = lax.broadcasted_iota(jnp.int32, (8, BLOCK), 0)
    row = lax.broadcasted_iota(jnp.int32, (8, CHUNK), 0)
    pair = lax.broadcasted_iota(jnp.int32, (1, CHUNK), 1)
    center = row.astype(F32) * SPACING
    gap = lax.rem(pair, BLOCK) - pair // BLOCK
    mates_blocks = own.at[pl.ds(0, members - 1)]
    mates_grads = grads.at[pl.ds(0, members - 1)]

    pltpu.make_async_copy(mates_blocks, mates_blocks, own_recv_sem).wait()
    lend.start()

    def group(turn, carry):
        which = jnp.where(early, 1 - turn, turn)

        @pl.when(which == 0)
        def _():
            ask.wait_recv()

        @pl.when(which == 1)
        def _():
            lend.wait_recv()

        spot = asked[which, BLOCK:ROWS, 0:BLOCK]
        scale8 = jnp.zeros((8, BLOCK), F32)
        for r in range(4):
            for s in range(4):
                there = (row8 == s) & (spot[3:4] == float(r))
                scale8 = jnp.where(there, scale_ref[r, s], scale8)
        small = jnp.concatenate(parts(spot, 3) + parts(scale8, 3), axis=0).astype(BF16)
        half_hi, half_lo = parts(radial_ref[...] * 0.5, 2)
        for k in range(PAIRS // CHUNK):
            mine = pl.ds(k * CENTRES, CENTRES)
            self_hi, self_lo = parts(asked[which, mine, :] * 0.5, 2)
            rest = [half_hi, half_lo, half_hi, jnp.zeros((8, C), F32), self_hi, self_lo]
            lhs_rest[k] = jnp.concatenate(rest, axis=0).T.astype(BF16)
            lanes = slice(k * CHUNK, (k + 1) * CHUNK)
            spread = dot(small, hot_centre[:, lanes])
            pos_exp[:, lanes] = spread[0:8] + spread[8:16] + spread[16:24]
            scale_exp[:, lanes] = spread[24:32] + spread[32:40] + spread[40:48]
        pair_acc[...] = jnp.zeros_like(pair_acc)

        def tile(slot, carry):
            @pl.when(early & (which == 1) & (slot == 1))
            def _():
                ask_far()

            hot_rows = pl.ds(pl.multiple_of(ROWS + slot * members, 8), members)
            near_rows = pl.ds(pl.multiple_of(ROWS + (slot + 3) * members, 8), members)
            hot = asked[which, hot_rows, :]
            live = jnp.sum(hot, axis=0, keepdims=True)
            self_hot = asked[which, pl.ds(ROWS + slot * members + me, 1), :]
            self_hot = jnp.where(which == 1, self_hot, 0.0)
            self_hot = jnp.concatenate([self_hot] * (CHUNK // C), axis=1)
            chosen = own[0] * hot[0:1]
            for k in range(1, members):
                chosen = chosen + own[k] * hot[k : k + 1]
            block_ref[0:ROWS, :] = chosen
            block_ref[ROWS:, :] = jnp.broadcast_to(live, (8, C))

            @pl.when(which == 1)
            def _():
                near_hot = asked[which, near_rows, :]
                chosen = block_ref[0:ROWS, :]
                for k in range(members):
                    chosen = chosen + near[k] * near_hot[k : k + 1]
                block_ref[0:ROWS, :] = chosen
                near_live = jnp.sum(near_hot, axis=0, keepdims=True)
                block_ref[ROWS:, :] += jnp.broadcast_to(near_live, (8, C))

            block = block_ref[0:ROWS, :]
            live = jnp.concatenate([block_ref[ROWS : ROWS + 1, :]] * (CHUNK // C), axis=1)
            place_j = jnp.concatenate([block[BLOCK:ROWS, 0:BLOCK]] * (CHUNK // BLOCK), axis=1)
            kind_hot = jnp.where(place_j[3:4] == row.astype(F32), 1.0, 0.0)
            lhs_send[...] = jnp.concatenate(parts(block[0:BLOCK] * 0.5, 2), axis=0).T.astype(BF16)

            def first(turn):
                lanes = slice(turn * CHUNK, (turn + 1) * CHUNK)
                diff = jnp.where(row < 3, place_j - pos_exp[:, lanes], 0.0)
                dist_sq = jnp.sum(diff * diff, axis=0, keepdims=True)
                scale = jnp.sum(scale_exp[:, lanes] * kind_hot, axis=0, keepdims=True)
                scaled = dist_sq * scale
                keep = live - jnp.where(gap == turn * CENTRES, self_hot, 0.0)
                reach = jnp.maximum(1.0 - scaled * (1.0 / 2.5), 0.0)
                offset = (scaled - center) * (1.0 / SPACING)
                basis = jnp.exp(-(offset * offset))
                slope = basis * offset * (-2.0 / SPACING)
                basis_hi, basis_lo = parts(basis, 2)
                head = jnp.concatenate(
                    [basis_hi, basis_hi, basis_lo, jnp.zeros((8, CHUNK), F32)], axis=0
                ).astype(BF16)
                rhs = jnp.concatenate([rhs_pair[...], head, rhs_centre[...]], axis=0)
                lhs = jnp.concatenate([lhs_send[...], lhs_rest[turn]], axis=1)
                return lanes, diff, scale, keep, reach, slope, dot(lhs, rhs)

            def second(state):
                half = state[-1]
                t = jnp.tanh(half)
                p = 1.0 + t
                hidden = half * p
                slope_1 = p + hidden * (1.0 - t)
                half = dot(lhs_m[...], hidden.astype(BF16))
                return state[:-1] + (slope_1, half)

            def third(state):
                half = state[-1]
                t = jnp.tanh(half)
                p = (1.0 + t) * jnp.concatenate([ro_exp[...]] * (CHUNK // C), axis=1)
                mixed = half * p
                slope_2 = p + mixed * (1.0 - t)
                out = dot(lhs_b[...], jnp.concatenate([mixed, slope_2], axis=0).astype(BF16))
                return state[:-1] + (out,)

            def fourth(state):
                lanes, diff, scale, keep, reach, slope, slope_1, out = state
                d_basis = dot(lhs_r[...], (out[0:C] * slope_1).astype(BF16))
                d_basis = d_basis[0:8] + d_basis[8:16]
                energy = out[C : C + 1]
                cut = reach * reach
                d_scaled = cut * jnp.sum(d_basis * slope, axis=0, keepdims=True)
                d_scaled = d_scaled - (2.0 / 2.5) * reach * energy
                force = (2.0 * keep * scale * d_scaled) * diff
                found = jnp.where(row == 3, keep * cut * energy, force)
                pair_acc[:, lanes] += found
                total = found[:, 0:C]
                for k in range(1, CHUNK // C):
                    total = total + found[:, k * C : (k + 1) * C]
                return total

            stages = [first, second, third, fourth]
            states = {}
            total = None
            count = PAIRS // CHUNK
            for turn in range(count + 3):
                for depth in range(4):
                    sub = turn - depth
                    if 0 <= sub < count:
                        states[sub] = stages[depth](states.get(sub, sub))
                        if depth == 3:
                            part = states.pop(sub)
                            total = part if total is None else total + part
            grad = total[:, 0:BLOCK] + total[:, BLOCK:C]
            grad = jnp.concatenate([grad, jnp.zeros_like(grad)], axis=1)
            for k in range(members):
                grads[k] += grad * hot[k : k + 1]

            @pl.when(which == 1)
            def _():
                near_hot = asked[which, near_rows, :]
                for k in range(members):
                    near_grads[k] += grad * near_hot[k : k + 1]

            return carry

        lax.fori_loop(0, 3, tile, 0)

        total = jnp.zeros((24, BLOCK), F32)
        for k in range(PAIRS // CHUNK):
            lanes = slice(k * CHUNK, (k + 1) * CHUNK)
            split = jnp.concatenate(parts(pair_acc[:, lanes], 3), axis=0).astype(BF16)
            total = total + lax.dot_general(
                split,
                hot_centre[:, lanes],
                (((1,), (1,)), ((), ())),
                preferred_element_type=F32,
            )
        total = total[0:8] + total[8:16] + total[16:24]
        centre_sums[which] = jnp.concatenate([total, jnp.zeros_like(total)], axis=1)

        @pl.when(which == 0)
        def _():
            tell.start()

        @pl.when(which == 1)
        def _():
            repay.start()

        return carry

    lax.fori_loop(0, 2, group, 0)

    repay.wait_recv()
    grads[...] += near_back[...]
    for mate in mates:
        pltpu.make_async_remote_copy(
            src_ref=grads.at[mate],
            dst_ref=back.at[me],
            send_sem=back_send_sem,
            recv_sem=back_recv_sem,
            device_id=(slab, mate),
            device_id_type=MESH,
        ).start()
    back[me] = grads[me]

    tell.wait_recv()
    centre_sum = centre_sums[1] + returned[...]
    energy_ref[...] = centre_sum[3:4, 0:BLOCK].reshape(BLOCK)
    pltpu.make_async_copy(mates_grads, mates_grads, back_recv_sem).wait()
    total = back[0]
    for k in range(1, members):
        total = total + back[k]
    force_ref[...] = (centre_sum - total)[0:3, 0:BLOCK]

    for sent in (ask, tell, lend, repay):
        sent.wait_send()
    pltpu.make_async_copy(mates_blocks, mates_blocks, own_send_sem).wait()
    pltpu.make_async_copy(mates_grads, mates_grads, back_send_sem).wait()


def solution(mesh):
    slabs, members = mesh.shape["slab"], mesh.shape["grp"]
    vmem = pl.BlockSpec(memory_space=pltpu.VMEM)
    call = pl.pallas_call(
        functools.partial(kernel, slabs, members),
        out_shape=(
            jax.ShapeDtypeStruct((BLOCK,), F32),
            jax.ShapeDtypeStruct((3, BLOCK), F32),
        ),
        in_specs=[pl.BlockSpec(memory_space=pltpu.HBM)] * 11,
        out_specs=(vmem, vmem),
        scratch_shapes=[
            pltpu.VMEM((3, BLOCK), F32),
            pltpu.VMEM((BLOCK,), jnp.int32),
            pltpu.VMEM((BLOCK, C), BF16),
            pltpu.VMEM((C, C), BF16),
            pltpu.VMEM((C, C), BF16),
            pltpu.VMEM((8, C), F32),
            pltpu.VMEM((C, C), BF16),
            pltpu.VMEM((C,), F32),
            pltpu.SMEM((4, 4), F32),
            pltpu.SMEM((1, 4), jnp.int32),
            pltpu.SMEM((1,), jnp.int32),
            pltpu.VMEM((members, ROWS, C), F32),
            pltpu.VMEM((members, ROWS, C), F32),
            pltpu.VMEM((2, ROWS + 6 * members, C), F32),
            pltpu.VMEM((ROWS + 3 * members, C), F32),
            pltpu.VMEM((ROWS + 8, C), F32),
            pltpu.VMEM((8, PAIRS), F32),
            pltpu.VMEM((8, PAIRS), F32),
            pltpu.VMEM((BLOCK, PAIRS), BF16),
            pltpu.VMEM((2 * BLOCK, CHUNK), BF16),
            pltpu.VMEM((2 * CENTRES, CHUNK), BF16),
            pltpu.VMEM((C, 2 * BLOCK), BF16),
            pltpu.VMEM((PAIRS // CHUNK, C, 32 + 2 * CENTRES), BF16),
            pltpu.VMEM((C + 16, 2 * C), BF16),
            pltpu.VMEM((16, C), BF16),
            pltpu.VMEM((C, C), BF16),
            pltpu.VMEM((C, C), F32),
            pltpu.VMEM((8, PAIRS), F32),
            pltpu.VMEM((2, 8, C), F32),
            pltpu.VMEM((members, 8, C), F32),
            pltpu.VMEM((members, 8, C), F32),
            pltpu.VMEM((members, 8, C), F32),
            pltpu.VMEM((8, C), F32),
            pltpu.VMEM((members, 8, C), F32),
            pltpu.SemaphoreType.DMA((11,)),
            pltpu.SemaphoreType.DMA((4,)),
            pltpu.SemaphoreType.DMA((4,)),
            pltpu.SemaphoreType.DMA,
            pltpu.SemaphoreType.DMA,
            pltpu.SemaphoreType.DMA,
            pltpu.SemaphoreType.DMA,
            pltpu.SemaphoreType.REGULAR,
            pltpu.SemaphoreType.REGULAR,
        ],
        compiler_params=pltpu.CompilerParams(
            collective_id=0, has_side_effects=True, vmem_limit_bytes=60 * 2**20
        ),
    )
    return jax.shard_map(
        call,
        mesh=mesh,
        in_specs=(
            P(None, ("slab", "grp")),
            P(("slab", "grp")),
            P(("slab", "grp"), None),
            P(),
            P(),
            P(),
            P(),
            P(),
            P(),
            P(("slab", "grp"), None),
            P(("slab", "grp")),
        ),
        out_specs=(P(("slab", "grp")), P(None, ("slab", "grp"))),
        check_vma=False,
    )
```

```python
import functools

import jax
import jax.numpy as jnp
from jax import lax
from jax.experimental import pallas as pl
from jax.experimental.pallas import tpu as pltpu
from jax.sharding import PartitionSpec as P

BLOCK = 64
C = 128
ROWS = 72
PAIRS = BLOCK * BLOCK
CHUNK = 1024
CENTRES = CHUNK // BLOCK
SPACING = 2.5 / 7
MESH = pl.DeviceIdType.MESH
BF16, F32 = jnp.bfloat16, jnp.float32


def parts(value, count):
    found = []
    for _ in range(count):
        part = value.astype(BF16).astype(F32)
        found.append(part)
        value = value - part
    return found


def dot(left, right):
    return jnp.dot(left, right, preferred_element_type=F32)


def centre_onehot(start, width):
    lane = lax.broadcasted_iota(jnp.int32, (BLOCK, width), 1) + start
    row = lax.broadcasted_iota(jnp.int32, (BLOCK, width), 0)
    return jnp.where((lane // BLOCK) == row, 1.0, 0.0).astype(F32)


def kernel(
    slabs,
    members,
    pos_hbm,
    spc_hbm,
    node_hbm,
    wself_hbm,
    wsend_hbm,
    radial_hbm,
    wmix_hbm,
    readout_hbm,
    scale_hbm,
    nbr_hbm,
    count_hbm,
    energy_ref,
    force_ref,
    pos_ref,
    spc_ref,
    node_ref,
    wself_ref,
    wsend_ref,
    radial_ref,
    wmix_ref,
    readout_ref,
    scale_ref,
    nbr_ref,
    count_ref,
    own,
    near,
    asked,
    centres,
    block_ref,
    pos_exp,
    scale_exp,
    hot_centre,
    rhs_pair,
    rhs_centre,
    lhs_send,
    lhs_rest,
    lhs_b,
    lhs_r,
    lhs_m,
    ro_exp,
    pair_acc,
    centre_sums,
    grads,
    near_grads,
    near_back,
    returned,
    back,
    load_sem,
    send_sem,
    recv_sem,
    own_send_sem,
    own_recv_sem,
    back_send_sem,
    back_recv_sem,
    group_sem,
):
    slab, me = lax.axis_index("slab"), lax.axis_index("grp")
    core = lax.rem(slab, 2)
    sib_slab = slab + 1 - 2 * core
    far_slab = lax.rem(slab - 1 + 2 * core + slabs, slabs)

    barrier = pltpu.get_barrier_semaphore()
    mates = [lax.rem(me + k, members) for k in range(1, members)]
    pl.semaphore_signal(barrier, inc=1, device_id=(far_slab, me), device_id_type=MESH)
    for mate in mates:
        pl.semaphore_signal(
            barrier, inc=1, device_id=(slab + 1 - core, mate), device_id_type=MESH
        )

    @pl.when(core == 0)
    def _():
        pl.semaphore_signal(barrier, inc=1, device_id=(sib_slab, me), device_id_type=MESH)

    loads = [
        pltpu.make_async_copy(source, target, load_sem.at[k])
        for k, (source, target) in enumerate(
            [
                (node_hbm, node_ref),
                (wself_hbm, wself_ref),
                (wsend_hbm, wsend_ref),
                (pos_hbm, pos_ref),
                (spc_hbm, spc_ref),
                (nbr_hbm, nbr_ref),
                (count_hbm, count_ref),
                (radial_hbm, radial_ref),
                (wmix_hbm, wmix_ref),
                (readout_hbm, readout_ref),
                (scale_hbm, scale_ref),
            ]
        )
    ]
    for load in loads:
        load.start()

    def spread_hot(step, carry):
        lanes = pl.ds(pl.multiple_of(step * CHUNK, CHUNK), CHUNK)
        hot_centre[:, lanes] = centre_onehot(step * CHUNK, CHUNK).astype(BF16)
        return carry

    for load in loads[:7]:
        load.wait()

    species = spc_ref[...].astype(F32).reshape(1, BLOCK)
    pad = jnp.zeros((1, BLOCK), F32)
    place = jnp.concatenate([pos_ref[...], species, pad, pad, pad, pad], axis=0)
    place = jnp.concatenate([place, jnp.zeros_like(place)], axis=1)
    features = dot(node_ref[...], wself_ref[...])
    own[me, 0:BLOCK, :] = dot(node_ref[...], wsend_ref[...])
    own[me, BLOCK:ROWS, :] = place
    asked_row = lax.broadcasted_iota(jnp.int32, (3 * members, C), 0)

    def slots_in(panel, first):
        hot = jnp.zeros((3 * members, C), F32)
        for k, slot in enumerate((first, 2, 3)):
            other = nbr_ref[0, slot]
            wanted = jnp.where(
                (other // members == panel) & (slot < count_ref[0]),
                lax.rem(other, members) + k * members,
                -1,
            )
            hot = jnp.where(asked_row == wanted, 1.0, hot)
        return hot

    centres[0:BLOCK, :] = features
    centres[BLOCK:ROWS, :] = place
    centres[ROWS:, :] = slots_in(2 * core, core)
    asked[1, 0:BLOCK, :] = features
    asked[1, BLOCK:ROWS, :] = place
    asked[1, ROWS : ROWS + 3 * members, :] = slots_in(1, 1 - core)
    asked[1, ROWS + 3 * members :, :] = slots_in(2 - 2 * core, 1 - core)

    @pl.when(core == 1)
    def _():
        pl.semaphore_wait(barrier, 2 * members)
        pl.semaphore_signal(group_sem, inc=1, device_id=(sib_slab, me), device_id_type=MESH)

    @pl.when(core == 0)
    def _():
        pl.semaphore_wait(group_sem, 1)

    for mate in mates:
        pltpu.make_async_remote_copy(
            src_ref=own.at[me],
            dst_ref=own.at[me],
            send_sem=own_send_sem,
            recv_sem=own_recv_sem,
            device_id=(slab, mate),
            device_id_type=MESH,
        ).start()

    def copy(index, source, target, to_slab):
        return pltpu.make_async_remote_copy(
            src_ref=source,
            dst_ref=target,
            send_sem=send_sem.at[index],
            recv_sem=recv_sem.at[index],
            device_id=(to_slab, me),
            device_id_type=MESH,
        )

    ask = copy(0, centres, asked.at[0, pl.ds(0, ROWS + 3 * members)], far_slab)
    tell = copy(1, centre_sums.at[0], returned, far_slab)
    lend = copy(2, own, near, sib_slab)
    repay = copy(3, near_grads, near_back, sib_slab)
    early = slab == 0

    def ask_far():
        @pl.when(core == 0)
        def _():
            pl.semaphore_wait(barrier, 1)

        ask.start()

    pl.when(jnp.logical_not(early))(ask_far)

    lax.fori_loop(0, PAIRS // CHUNK, spread_hot, 0)
    atom = lax.broadcasted_iota(jnp.int32, (BLOCK, CHUNK), 0)
    lane = lax.broadcasted_iota(jnp.int32, (BLOCK, CHUNK), 1)
    hot_j = jnp.where(lax.rem(lane, BLOCK) == atom, 1.0, 0.0).astype(F32)
    rhs_pair[...] = jnp.concatenate([hot_j, hot_j], axis=0).astype(BF16)
    hot_i = centre_onehot(0, CHUNK)[0:CENTRES]
    rhs_centre[...] = jnp.concatenate([hot_i, hot_i], axis=0).astype(BF16)
    for load in loads[7:]:
        load.wait()
    radial_hi, radial_lo = parts(radial_ref[...], 2)
    lhs_r[...] = (jnp.concatenate([radial_hi, radial_lo], axis=0) * 0.25).astype(BF16)
    lhs_m[...] = (wmix_ref[...].astype(F32).T * 0.5).astype(BF16)
    ones = jnp.ones((16, C), F32)
    lhs_b[...] = jnp.concatenate(
        [
            jnp.concatenate([jnp.zeros((C, C), F32), ones], axis=0),
            jnp.concatenate([wmix_ref[...].astype(F32), jnp.zeros((16, C), F32)], axis=0),
        ],
        axis=1,
    ).astype(BF16)
    readout = readout_ref[...].reshape(1, C)
    ro_exp[...] = jnp.broadcast_to(readout, (C, C)).T
    grads[...] = jnp.zeros_like(grads)
    near_grads[...] = jnp.zeros_like(near_grads)

    row8 = lax.broadcasted_iota(jnp.int32, (8, BLOCK), 0)
    row = lax.broadcasted_iota(jnp.int32, (8, CHUNK), 0)
    pair = lax.broadcasted_iota(jnp.int32, (1, CHUNK), 1)
    center = row.astype(F32) * SPACING
    gap = lax.rem(pair, BLOCK) - pair // BLOCK
    mates_blocks = own.at[pl.ds(0, members - 1)]
    mates_grads = grads.at[pl.ds(0, members - 1)]

    pltpu.make_async_copy(mates_blocks, mates_blocks, own_recv_sem).wait()
    lend.start()

    def group(turn, carry):
        which = jnp.where(early, 1 - turn, turn)

        @pl.when(which == 0)
        def _():
            ask.wait_recv()

        @pl.when(which == 1)
        def _():
            lend.wait_recv()

        spot = asked[which, BLOCK:ROWS, 0:BLOCK]
        scale8 = jnp.zeros((8, BLOCK), F32)
        for r in range(4):
            for s in range(4):
                there = (row8 == s) & (spot[3:4] == float(r))
                scale8 = jnp.where(there, scale_ref[r, s], scale8)
        small = jnp.concatenate(parts(spot, 3) + parts(scale8, 3), axis=0).astype(BF16)
        half_hi, half_lo = parts(radial_ref[...] * 0.5, 2)
        for k in range(PAIRS // CHUNK):
            mine = pl.ds(k * CENTRES, CENTRES)
            self_hi, self_lo = parts(asked[which, mine, :] * 0.5, 2)
            rest = [half_hi, half_lo, half_hi, jnp.zeros((8, C), F32), self_hi, self_lo]
            lhs_rest[k] = jnp.concatenate(rest, axis=0).T.astype(BF16)
            lanes = slice(k * CHUNK, (k + 1) * CHUNK)
            spread = dot(small, hot_centre[:, lanes])
            pos_exp[:, lanes] = spread[0:8] + spread[8:16] + spread[16:24]
            scale_exp[:, lanes] = spread[24:32] + spread[32:40] + spread[40:48]
        pair_acc[...] = jnp.zeros_like(pair_acc)

        def tile(slot, carry):
            @pl.when(early & (which == 1) & (slot == 1))
            def _():
                ask_far()

            hot_rows = pl.ds(pl.multiple_of(ROWS + slot * members, 8), members)
            near_rows = pl.ds(pl.multiple_of(ROWS + (slot + 3) * members, 8), members)
            hot = asked[which, hot_rows, :]
            live = jnp.sum(hot, axis=0, keepdims=True)
            self_hot = asked[which, pl.ds(ROWS + slot * members + me, 1), :]
            self_hot = jnp.where(which == 1, self_hot, 0.0)
            self_hot = jnp.concatenate([self_hot] * (CHUNK // C), axis=1)
            chosen = own[0] * hot[0:1]
            for k in range(1, members):
                chosen = chosen + own[k] * hot[k : k + 1]
            block_ref[0:ROWS, :] = chosen
            block_ref[ROWS:, :] = jnp.broadcast_to(live, (8, C))

            @pl.when(which == 1)
            def _():
                near_hot = asked[which, near_rows, :]
                chosen = block_ref[0:ROWS, :]
                for k in range(members):
                    chosen = chosen + near[k] * near_hot[k : k + 1]
                block_ref[0:ROWS, :] = chosen
                near_live = jnp.sum(near_hot, axis=0, keepdims=True)
                block_ref[ROWS:, :] += jnp.broadcast_to(near_live, (8, C))

            block = block_ref[0:ROWS, :]
            live = jnp.concatenate([block_ref[ROWS : ROWS + 1, :]] * (CHUNK // C), axis=1)
            place_j = jnp.concatenate([block[BLOCK:ROWS, 0:BLOCK]] * (CHUNK // BLOCK), axis=1)
            kind_hot = jnp.where(place_j[3:4] == row.astype(F32), 1.0, 0.0)
            lhs_send[...] = jnp.concatenate(parts(block[0:BLOCK] * 0.5, 2), axis=0).T.astype(BF16)

            def first(turn):
                lanes = slice(turn * CHUNK, (turn + 1) * CHUNK)
                diff = jnp.where(row < 3, place_j - pos_exp[:, lanes], 0.0)
                dist_sq = jnp.sum(diff * diff, axis=0, keepdims=True)
                scale = jnp.sum(scale_exp[:, lanes] * kind_hot, axis=0, keepdims=True)
                scaled = dist_sq * scale
                keep = live - jnp.where(gap == turn * CENTRES, self_hot, 0.0)
                reach = jnp.maximum(1.0 - scaled * (1.0 / 2.5), 0.0)
                offset = (scaled - center) * (1.0 / SPACING)
                basis = jnp.exp(-(offset * offset))
                slope = basis * offset * (-2.0 / SPACING)
                basis_hi, basis_lo = parts(basis, 2)
                head = jnp.concatenate(
                    [basis_hi, basis_hi, basis_lo, jnp.zeros((8, CHUNK), F32)], axis=0
                ).astype(BF16)
                rhs = jnp.concatenate([rhs_pair[...], head, rhs_centre[...]], axis=0)
                lhs = jnp.concatenate([lhs_send[...], lhs_rest[turn]], axis=1)
                return lanes, diff, scale, keep, reach, slope, dot(lhs, rhs)

            def second(state):
                half = state[-1]
                t = jnp.tanh(half)
                p = 1.0 + t
                hidden = half * p
                slope_1 = p + hidden * (1.0 - t)
                half = dot(lhs_m[...], hidden.astype(BF16))
                return state[:-1] + (slope_1, half)

            def third(state):
                half = state[-1]
                t = jnp.tanh(half)
                p = (1.0 + t) * jnp.concatenate([ro_exp[...]] * (CHUNK // C), axis=1)
                mixed = half * p
                slope_2 = p + mixed * (1.0 - t)
                out = dot(lhs_b[...], jnp.concatenate([mixed, slope_2], axis=0).astype(BF16))
                return state[:-1] + (out,)

            def fourth(state):
                lanes, diff, scale, keep, reach, slope, slope_1, out = state
                d_basis = dot(lhs_r[...], (out[0:C] * slope_1).astype(BF16))
                d_basis = d_basis[0:8] + d_basis[8:16]
                energy = out[C : C + 1]
                cut = reach * reach
                d_scaled = cut * jnp.sum(d_basis * slope, axis=0, keepdims=True)
                d_scaled = d_scaled - (2.0 / 2.5) * reach * energy
                force = (2.0 * keep * scale * d_scaled) * diff
                found = jnp.where(row == 3, keep * cut * energy, force)
                pair_acc[:, lanes] += found
                total = found[:, 0:C]
                for k in range(1, CHUNK // C):
                    total = total + found[:, k * C : (k + 1) * C]
                return total

            stages = [first, second, third, fourth]
            states = {}
            total = None
            count = PAIRS // CHUNK
            for turn in range(count + 3):
                for depth in range(4):
                    sub = turn - depth
                    if 0 <= sub < count:
                        states[sub] = stages[depth](states.get(sub, sub))
                        if depth == 3:
                            part = states.pop(sub)
                            total = part if total is None else total + part
            grad = total[:, 0:BLOCK] + total[:, BLOCK:C]
            grad = jnp.concatenate([grad, jnp.zeros_like(grad)], axis=1)
            for k in range(members):
                grads[k] += grad * hot[k : k + 1]

            @pl.when(which == 1)
            def _():
                near_hot = asked[which, near_rows, :]
                for k in range(members):
                    near_grads[k] += grad * near_hot[k : k + 1]

            return carry

        lax.fori_loop(0, 3, tile, 0)

        total = jnp.zeros((24, BLOCK), F32)
        for k in range(PAIRS // CHUNK):
            lanes = slice(k * CHUNK, (k + 1) * CHUNK)
            split = jnp.concatenate(parts(pair_acc[:, lanes], 3), axis=0).astype(BF16)
            total = total + lax.dot_general(
                split,
                hot_centre[:, lanes],
                (((1,), (1,)), ((), ())),
                preferred_element_type=F32,
            )
        total = total[0:8] + total[8:16] + total[16:24]
        centre_sums[which] = jnp.concatenate([total, jnp.zeros_like(total)], axis=1)

        @pl.when(which == 0)
        def _():
            tell.start()

        @pl.when(which == 1)
        def _():
            repay.start()

        return carry

    lax.fori_loop(0, 2, group, 0)

    repay.wait_recv()
    grads[...] += near_back[...]
    for mate in mates:
        pltpu.make_async_remote_copy(
            src_ref=grads.at[mate],
            dst_ref=back.at[me],
            send_sem=back_send_sem,
            recv_sem=back_recv_sem,
            device_id=(slab, mate),
            device_id_type=MESH,
        ).start()
    back[me] = grads[me]

    tell.wait_recv()
    centre_sum = centre_sums[1] + returned[...]
    energy_ref[...] = centre_sum[3:4, 0:BLOCK].reshape(BLOCK)
    pltpu.make_async_copy(mates_grads, mates_grads, back_recv_sem).wait()
    total = back[0]
    for k in range(1, members):
        total = total + back[k]
    force_ref[...] = (centre_sum - total)[0:3, 0:BLOCK]

    for sent in (ask, tell, lend, repay):
        sent.wait_send()
    pltpu.make_async_copy(mates_blocks, mates_blocks, own_send_sem).wait()
    pltpu.make_async_copy(mates_grads, mates_grads, back_send_sem).wait()


def solution(mesh):
    slabs, members = mesh.shape["slab"], mesh.shape["grp"]
    vmem = pl.BlockSpec(memory_space=pltpu.VMEM)
    call = pl.pallas_call(
        functools.partial(kernel, slabs, members),
        out_shape=(
            jax.ShapeDtypeStruct((BLOCK,), F32),
            jax.ShapeDtypeStruct((3, BLOCK), F32),
        ),
        in_specs=[pl.BlockSpec(memory_space=pltpu.HBM)] * 11,
        out_specs=(vmem, vmem),
        scratch_shapes=[
            pltpu.VMEM((3, BLOCK), F32),
            pltpu.VMEM((BLOCK,), jnp.int32),
            pltpu.VMEM((BLOCK, C), BF16),
            pltpu.VMEM((C, C), BF16),
            pltpu.VMEM((C, C), BF16),
            pltpu.VMEM((8, C), F32),
            pltpu.VMEM((C, C), BF16),
            pltpu.VMEM((C,), F32),
            pltpu.SMEM((4, 4), F32),
            pltpu.SMEM((1, 4), jnp.int32),
            pltpu.SMEM((1,), jnp.int32),
            pltpu.VMEM((members, ROWS, C), F32),
            pltpu.VMEM((members, ROWS, C), F32),
            pltpu.VMEM((2, ROWS + 6 * members, C), F32),
            pltpu.VMEM((ROWS + 3 * members, C), F32),
            pltpu.VMEM((ROWS + 8, C), F32),
            pltpu.VMEM((8, PAIRS), F32),
            pltpu.VMEM((8, PAIRS), F32),
            pltpu.VMEM((BLOCK, PAIRS), BF16),
            pltpu.VMEM((2 * BLOCK, CHUNK), BF16),
            pltpu.VMEM((2 * CENTRES, CHUNK), BF16),
            pltpu.VMEM((C, 2 * BLOCK), BF16),
            pltpu.VMEM((PAIRS // CHUNK, C, 32 + 2 * CENTRES), BF16),
            pltpu.VMEM((C + 16, 2 * C), BF16),
            pltpu.VMEM((16, C), BF16),
            pltpu.VMEM((C, C), BF16),
            pltpu.VMEM((C, C), F32),
            pltpu.VMEM((8, PAIRS), F32),
            pltpu.VMEM((2, 8, C), F32),
            pltpu.VMEM((members, 8, C), F32),
            pltpu.VMEM((members, 8, C), F32),
            pltpu.VMEM((members, 8, C), F32),
            pltpu.VMEM((8, C), F32),
            pltpu.VMEM((members, 8, C), F32),
            pltpu.SemaphoreType.DMA((11,)),
            pltpu.SemaphoreType.DMA((4,)),
            pltpu.SemaphoreType.DMA((4,)),
            pltpu.SemaphoreType.DMA,
            pltpu.SemaphoreType.DMA,
            pltpu.SemaphoreType.DMA,
            pltpu.SemaphoreType.DMA,
            pltpu.SemaphoreType.REGULAR,
        ],
        compiler_params=pltpu.CompilerParams(
            collective_id=0, has_side_effects=True, vmem_limit_bytes=60 * 2**20
        ),
    )
    return jax.shard_map(
        call,
        mesh=mesh,
        in_specs=(
            P(None, ("slab", "grp")),
            P(("slab", "grp")),
            P(("slab", "grp"), None),
            P(),
            P(),
            P(),
            P(),
            P(),
            P(),
            P(("slab", "grp"), None),
            P(("slab", "grp")),
        ),
        out_specs=(P(("slab", "grp")), P(None, ("slab", "grp"))),
        check_vma=False,
    )
```

```python
import functools

import jax
import jax.numpy as jnp
from jax import lax
from jax.experimental import pallas as pl
from jax.experimental.pallas import tpu as pltpu
from jax.sharding import PartitionSpec as P

BLOCK = 64
C = 128
ROWS = 72
PAIRS = BLOCK * BLOCK
CHUNK = 1024
CENTRES = CHUNK // BLOCK
SPACING = 2.5 / 7
ROWS_OF_PAIRS = PAIRS // 128
ROOT = 1.4426950408889634**0.5
MESH = pl.DeviceIdType.MESH
BF16, F32 = jnp.bfloat16, jnp.float32


def parts(value, count):
    found = []
    for _ in range(count):
        part = value.astype(BF16).astype(F32)
        found.append(part)
        value = value - part
    return found


def dot(left, right):
    return jnp.dot(left, right, preferred_element_type=F32)


def centre_onehot(start, width):
    lane = lax.broadcasted_iota(jnp.int32, (BLOCK, width), 1) + start
    row = lax.broadcasted_iota(jnp.int32, (BLOCK, width), 0)
    return jnp.where((lane // BLOCK) == row, 1.0, 0.0).astype(F32)


def kernel(
    slabs,
    members,
    pos_hbm,
    spc_hbm,
    node_hbm,
    wself_hbm,
    wsend_hbm,
    radial_hbm,
    wmix_hbm,
    readout_hbm,
    scale_hbm,
    nbr_hbm,
    count_hbm,
    energy_ref,
    force_ref,
    pos_ref,
    spc_ref,
    node_ref,
    wself_ref,
    wsend_ref,
    radial_ref,
    wmix_ref,
    readout_ref,
    scale_ref,
    nbr_ref,
    count_ref,
    own,
    near,
    asked,
    centres,
    spread,
    scaled_ref,
    slope_ref,
    energy_rows,
    rhs_pair,
    rhs_centre,
    lhs_send,
    lhs_rest,
    lhs_b,
    lhs_r,
    lhs_m,
    ro_exp,
    pair_acc,
    centre_sums,
    grads,
    near_grads,
    near_back,
    returned,
    back,
    load_sem,
    send_sem,
    recv_sem,
    own_send_sem,
    own_recv_sem,
    back_send_sem,
    back_recv_sem,
    group_sem,
):
    slab, me = lax.axis_index("slab"), lax.axis_index("grp")
    core = lax.rem(slab, 2)
    sib_slab = slab + 1 - 2 * core
    far_slab = lax.rem(slab - 1 + 2 * core + slabs, slabs)

    barrier = pltpu.get_barrier_semaphore()
    mates = [lax.rem(me + k, members) for k in range(1, members)]
    pl.semaphore_signal(barrier, inc=1, device_id=(far_slab, me), device_id_type=MESH)
    for mate in mates:
        pl.semaphore_signal(
            barrier, inc=1, device_id=(slab + 1 - core, mate), device_id_type=MESH
        )

    @pl.when(core == 0)
    def _():
        pl.semaphore_signal(barrier, inc=1, device_id=(sib_slab, me), device_id_type=MESH)

    loads = [
        pltpu.make_async_copy(source, target, load_sem.at[k])
        for k, (source, target) in enumerate(
            [
                (node_hbm, node_ref),
                (wself_hbm, wself_ref),
                (wsend_hbm, wsend_ref),
                (pos_hbm, pos_ref),
                (spc_hbm, spc_ref),
                (nbr_hbm, nbr_ref),
                (count_hbm, count_ref),
                (radial_hbm, radial_ref),
                (wmix_hbm, wmix_ref),
                (readout_hbm, readout_ref),
                (scale_hbm, scale_ref),
            ]
        )
    ]
    for load in loads:
        load.start()

    for load in loads[:7]:
        load.wait()

    species = spc_ref[...].astype(F32).reshape(1, BLOCK)
    pad = jnp.zeros((1, BLOCK), F32)
    place = jnp.concatenate([pos_ref[...], species, pad, pad, pad, pad], axis=0)
    place = jnp.concatenate([place, jnp.zeros_like(place)], axis=1)
    features = dot(node_ref[...], wself_ref[...])
    own[me, 0:BLOCK, :] = dot(node_ref[...], wsend_ref[...])
    own[me, BLOCK:ROWS, :] = place
    asked_row = lax.broadcasted_iota(jnp.int32, (3 * members, C), 0)

    def slots_in(panel, first):
        hot = jnp.zeros((3 * members, C), F32)
        for k, slot in enumerate((first, 2, 3)):
            other = nbr_ref[0, slot]
            wanted = jnp.where(
                (other // members == panel) & (slot < count_ref[0]),
                lax.rem(other, members) + k * members,
                -1,
            )
            hot = jnp.where(asked_row == wanted, 1.0, hot)
        return hot

    centres[0:BLOCK, :] = features
    centres[BLOCK:ROWS, :] = place
    centres[ROWS:, :] = slots_in(2 * core, core)
    asked[1, 0:BLOCK, :] = features
    asked[1, BLOCK:ROWS, :] = place
    asked[1, ROWS : ROWS + 3 * members, :] = slots_in(1, 1 - core)
    asked[1, ROWS + 3 * members :, :] = slots_in(2 - 2 * core, 1 - core)
    asked[0, ROWS + 3 * members :, :] = jnp.zeros((3 * members, C), F32)

    @pl.when(core == 1)
    def _():
        pl.semaphore_wait(barrier, 2 * members)
        pl.semaphore_signal(group_sem, inc=1, device_id=(sib_slab, me), device_id_type=MESH)

    @pl.when(core == 0)
    def _():
        pl.semaphore_wait(group_sem, 1)

    for mate in mates:
        pltpu.make_async_remote_copy(
            src_ref=own.at[me],
            dst_ref=own.at[me],
            send_sem=own_send_sem,
            recv_sem=own_recv_sem,
            device_id=(slab, mate),
            device_id_type=MESH,
        ).start()

    def copy(index, source, target, to_slab):
        return pltpu.make_async_remote_copy(
            src_ref=source,
            dst_ref=target,
            send_sem=send_sem.at[index],
            recv_sem=recv_sem.at[index],
            device_id=(to_slab, me),
            device_id_type=MESH,
        )

    ask = copy(0, centres, asked.at[0, pl.ds(0, ROWS + 3 * members)], far_slab)
    tell = copy(1, centre_sums.at[0], returned, far_slab)
    lend = copy(2, own, near, sib_slab)
    repay = copy(3, near_grads, near_back, sib_slab)
    early = slab == 0

    def ask_far():
        @pl.when(core == 0)
        def _():
            pl.semaphore_wait(barrier, 1)

        ask.start()

    pl.when(jnp.logical_not(early))(ask_far)

    atom = lax.broadcasted_iota(jnp.int32, (BLOCK, CHUNK), 0)
    lane = lax.broadcasted_iota(jnp.int32, (BLOCK, CHUNK), 1)
    hot_j = jnp.where(lax.rem(lane, BLOCK) == atom, 1.0, 0.0).astype(F32)
    rhs_pair[...] = jnp.concatenate([hot_j, hot_j], axis=0).astype(BF16)
    hot_i = centre_onehot(0, CHUNK)[0:CENTRES]
    rhs_centre[...] = jnp.concatenate([hot_i, hot_i], axis=0).astype(BF16)
    for load in loads[7:]:
        load.wait()
    radial_hi, radial_lo = parts(radial_ref[...], 2)
    lhs_r[...] = (jnp.concatenate([radial_hi, radial_lo], axis=0) * 0.25).astype(BF16)
    lhs_m[...] = (wmix_ref[...].astype(F32).T * 0.5).astype(BF16)
    ones = jnp.ones((16, C), F32)
    lhs_b[...] = jnp.concatenate(
        [
            jnp.concatenate([jnp.zeros((C, C), F32), ones], axis=0),
            jnp.concatenate([wmix_ref[...].astype(F32), jnp.zeros((16, C), F32)], axis=0),
        ],
        axis=1,
    ).astype(BF16)
    readout = readout_ref[...].reshape(1, C)
    ro_exp[...] = jnp.broadcast_to(readout, (C, C)).T
    grads[...] = jnp.zeros_like(grads)
    near_grads[...] = jnp.zeros_like(near_grads)

    row8 = lax.broadcasted_iota(jnp.int32, (8, BLOCK), 0)
    center = lax.broadcasted_iota(jnp.int32, (8, CHUNK), 0).astype(F32) * ROOT
    line = lax.broadcasted_iota(jnp.int32, (ROWS_OF_PAIRS, BLOCK), 0)
    atom = lax.broadcasted_iota(jnp.int32, (ROWS_OF_PAIRS, BLOCK), 1)
    on_line = jnp.where(atom // 2 == line, 1.0, 0.0)
    lane = lax.broadcasted_iota(jnp.int32, (BLOCK, C), 1)
    atom = lax.broadcasted_iota(jnp.int32, (BLOCK, C), 0)
    in_half = jnp.where(lax.rem(atom, 2) == lane // BLOCK, 1.0, 0.0).astype(BF16)
    line = lax.broadcasted_iota(jnp.int32, (ROWS_OF_PAIRS, C), 0)
    lane = lax.broadcasted_iota(jnp.int32, (ROWS_OF_PAIRS, C), 1)
    same_atom = jnp.where(2 * line + lane // BLOCK == lax.rem(lane, BLOCK), 1.0, 0.0)
    mates_blocks = own.at[pl.ds(0, members - 1)]
    mates_grads = grads.at[pl.ds(0, members - 1)]

    pltpu.make_async_copy(mates_blocks, mates_blocks, own_recv_sem).wait()
    lend.start()
    lend.wait_recv()

    def group(turn, carry):
        which = jnp.where(early, 1 - turn, turn)

        @pl.when(which == 0)
        def _():
            ask.wait_recv()

        spot = asked[which, BLOCK:ROWS, 0:BLOCK]
        scale8 = jnp.zeros((8, BLOCK), F32)
        for r in range(4):
            for s in range(4):
                there = (row8 == s) & (spot[3:4] == float(r))
                scale8 = jnp.where(there, scale_ref[r, s], scale8)
        wide = []
        for values in [spot[k : k + 1] for k in range(3)] + [scale8[k : k + 1] for k in range(4)]:
            wide += [on_line * part for part in parts(values, 3)]
        found = dot(jnp.concatenate(wide, axis=0).astype(BF16), in_half)
        for k in range(7):
            base = k * 3 * ROWS_OF_PAIRS
            one, two, three = (
                found[base + p * ROWS_OF_PAIRS : base + (p + 1) * ROWS_OF_PAIRS] for p in range(3)
            )
            spread[k] = one + two + three
        half_hi, half_lo = parts(radial_ref[...] * 0.5, 2)
        for k in range(PAIRS // CHUNK):
            mine = pl.ds(k * CENTRES, CENTRES)
            self_hi, self_lo = parts(asked[which, mine, :] * 0.5, 2)
            rest = [half_hi, half_lo, half_hi, jnp.zeros((8, C), F32), self_hi, self_lo]
            lhs_rest[k] = jnp.concatenate(rest, axis=0).T.astype(BF16)
        pair_acc[...] = jnp.zeros_like(pair_acc)

        def tile(slot, carry):
            @pl.when(early & (which == 1) & (slot == 0))
            def _():
                ask_far()

            hot_rows = pl.ds(pl.multiple_of(ROWS + slot * members, 8), members)
            near_rows = pl.ds(pl.multiple_of(ROWS + (slot + 3) * members, 8), members)
            hot = asked[which, hot_rows, :]
            near_hot = asked[which, near_rows, :]
            live = jnp.sum(hot + near_hot, axis=0, keepdims=True)
            self_hot = asked[which, pl.ds(ROWS + slot * members + me, 1), :]
            self_hot = jnp.where(which == 1, self_hot, 0.0)
            block = own[0] * hot[0:1] + near[0] * near_hot[0:1]
            for k in range(1, members):
                block = block + own[k] * hot[k : k + 1] + near[k] * near_hot[k : k + 1]
            lhs_send[...] = jnp.concatenate(parts(block[0:BLOCK] * 0.5, 2), axis=0).T.astype(BF16)
            place_j = block[BLOCK:ROWS, 0:BLOCK]
            place_j = jnp.concatenate([place_j, place_j], axis=1)
            diff = [place_j[k : k + 1] - spread[k] for k in range(3)]
            dist_sq = diff[0] * diff[0] + diff[1] * diff[1] + diff[2] * diff[2]
            kind = place_j[3:4]
            scale = jnp.where(
                kind == 0.0,
                spread[3],
                jnp.where(kind == 1.0, spread[4], jnp.where(kind == 2.0, spread[5], spread[6])),
            )
            scaled = dist_sq * scale
            scaled_ref[...] = scaled * (ROOT / SPACING)
            keep = live - self_hot * same_atom
            reach = jnp.maximum(1.0 - scaled * (1.0 / 2.5), 0.0)

            def first(turn):
                base = turn * (CHUNK // C)
                wide = [scaled_ref[base + k : base + k + 1, :] for k in range(CHUNK // C)]
                offset = jnp.concatenate(wide, axis=1) - center
                basis = jnp.exp2(-(offset * offset))
                slope = basis * offset
                basis_hi, basis_lo = parts(basis, 2)
                head = jnp.concatenate(
                    [basis_hi, basis_hi, basis_lo, jnp.zeros((8, CHUNK), F32)], axis=0
                ).astype(BF16)
                rhs = jnp.concatenate([rhs_pair[...], head, rhs_centre[...]], axis=0)
                lhs = jnp.concatenate([lhs_send[...], lhs_rest[turn]], axis=1)
                return base, slope, dot(lhs, rhs)

            def second(state):
                half = state[-1]
                t = jnp.tanh(half)
                p = 1.0 + t
                hidden = half * p
                slope_1 = p + hidden * (1.0 - t)
                half = dot(lhs_m[...], hidden.astype(BF16))
                return state[:-1] + (slope_1, half)

            def third(state):
                half = state[-1]
                t = jnp.tanh(half)
                p = (1.0 + t) * jnp.concatenate([ro_exp[...]] * (CHUNK // C), axis=1)
                mixed = half * p
                mixed = mixed.astype(BF16)
                slope_2 = p.astype(BF16) + mixed * (1.0 - t.astype(BF16))
                out = dot(lhs_b[...], jnp.concatenate([mixed, slope_2], axis=0))
                return state[:-1] + (out,)

            def fourth(state):
                base, slope, slope_1, out = state
                d_basis = dot(lhs_r[...], (out[0:C] * slope_1).astype(BF16))
                slope = jnp.sum((d_basis[0:8] + d_basis[8:16]) * slope, axis=0, keepdims=True)
                for k in range(CHUNK // C):
                    lanes = slice(k * C, (k + 1) * C)
                    slope_ref[base + k : base + k + 1, :] = slope[:, lanes]
                    energy_rows[base + k : base + k + 1, :] = out[C : C + 1, lanes]

            stages = [first, second, third, fourth]
            states = {}
            count = PAIRS // CHUNK
            for turn in range(count + 3):
                for depth in range(4):
                    sub = turn - depth
                    if 0 <= sub < count:
                        states[sub] = stages[depth](states.get(sub, sub))
            energy = energy_rows[...]
            cut = reach * reach
            d_scaled = cut * slope_ref[...] * (-2.0 / (SPACING * ROOT))
            d_scaled = 2.0 * keep * scale * (d_scaled - (2.0 / 2.5) * reach * energy)
            found = [d_scaled * part for part in diff]
            for k in range(3):
                pair_acc[k] += found[k]
            pair_acc[3] += keep * cut * energy
            total = [jnp.sum(part, axis=0, keepdims=True) for part in found]
            total = jnp.concatenate(total + [jnp.zeros((5, C), F32)], axis=0)
            grad = total[:, 0:BLOCK] + total[:, BLOCK:C]
            grad = jnp.concatenate([grad, jnp.zeros_like(grad)], axis=1)
            for k in range(members):
                grads[k] += grad * hot[k : k + 1]

            @pl.when(which == 1)
            def _():
                for k in range(members):
                    near_grads[k] += grad * near_hot[k : k + 1]

            return carry

        lax.fori_loop(0, 3, tile, 0)

        wide = []
        for k in range(4):
            wide += parts(pair_acc[k], 3)
        found = lax.dot_general(
            jnp.concatenate(wide, axis=0).astype(BF16),
            in_half,
            (((1,), (1,)), ((), ())),
            preferred_element_type=F32,
        )
        total = []
        for k in range(4):
            base = k * 3 * ROWS_OF_PAIRS
            one, two, three = (
                found[base + p * ROWS_OF_PAIRS : base + (p + 1) * ROWS_OF_PAIRS] for p in range(3)
            )
            total.append(jnp.sum((one + two + three) * on_line, axis=0, keepdims=True))
        total = jnp.concatenate(total + [jnp.zeros((4, BLOCK), F32)], axis=0)
        centre_sums[which] = jnp.concatenate([total, jnp.zeros_like(total)], axis=1)

        @pl.when(which == 0)
        def _():
            tell.start()

        @pl.when(which == 1)
        def _():
            repay.start()

        return carry

    lax.fori_loop(0, 2, group, 0)

    repay.wait_recv()
    grads[...] += near_back[...]
    for mate in mates:
        pltpu.make_async_remote_copy(
            src_ref=grads.at[mate],
            dst_ref=back.at[me],
            send_sem=back_send_sem,
            recv_sem=back_recv_sem,
            device_id=(slab, mate),
            device_id_type=MESH,
        ).start()
    back[me] = grads[me]

    tell.wait_recv()
    centre_sum = centre_sums[1] + returned[...]
    energy_ref[...] = centre_sum[3:4, 0:BLOCK].reshape(BLOCK)
    pltpu.make_async_copy(mates_grads, mates_grads, back_recv_sem).wait()
    total = back[0]
    for k in range(1, members):
        total = total + back[k]
    force_ref[...] = (centre_sum - total)[0:3, 0:BLOCK]

    for sent in (ask, tell, lend, repay):
        sent.wait_send()
    pltpu.make_async_copy(mates_blocks, mates_blocks, own_send_sem).wait()
    pltpu.make_async_copy(mates_grads, mates_grads, back_send_sem).wait()


def solution(mesh):
    slabs, members = mesh.shape["slab"], mesh.shape["grp"]
    vmem = pl.BlockSpec(memory_space=pltpu.VMEM)
    call = pl.pallas_call(
        functools.partial(kernel, slabs, members),
        out_shape=(
            jax.ShapeDtypeStruct((BLOCK,), F32),
            jax.ShapeDtypeStruct((3, BLOCK), F32),
        ),
        in_specs=[pl.BlockSpec(memory_space=pltpu.HBM)] * 11,
        out_specs=(vmem, vmem),
        scratch_shapes=[
            pltpu.VMEM((3, BLOCK), F32),
            pltpu.VMEM((BLOCK,), jnp.int32),
            pltpu.VMEM((BLOCK, C), BF16),
            pltpu.VMEM((C, C), BF16),
            pltpu.VMEM((C, C), BF16),
            pltpu.VMEM((8, C), F32),
            pltpu.VMEM((C, C), BF16),
            pltpu.VMEM((C,), F32),
            pltpu.SMEM((4, 4), F32),
            pltpu.SMEM((1, 4), jnp.int32),
            pltpu.SMEM((1,), jnp.int32),
            pltpu.VMEM((members, ROWS, C), F32),
            pltpu.VMEM((members, ROWS, C), F32),
            pltpu.VMEM((2, ROWS + 6 * members, C), F32),
            pltpu.VMEM((ROWS + 3 * members, C), F32),
            pltpu.VMEM((7, ROWS_OF_PAIRS, C), F32),
            pltpu.VMEM((ROWS_OF_PAIRS, C), F32),
            pltpu.VMEM((ROWS_OF_PAIRS, C), F32),
            pltpu.VMEM((ROWS_OF_PAIRS, C), F32),
            pltpu.VMEM((2 * BLOCK, CHUNK), BF16),
            pltpu.VMEM((2 * CENTRES, CHUNK), BF16),
            pltpu.VMEM((C, 2 * BLOCK), BF16),
            pltpu.VMEM((PAIRS // CHUNK, C, 32 + 2 * CENTRES), BF16),
            pltpu.VMEM((C + 16, 2 * C), BF16),
            pltpu.VMEM((16, C), BF16),
            pltpu.VMEM((C, C), BF16),
            pltpu.VMEM((C, C), F32),
            pltpu.VMEM((4, ROWS_OF_PAIRS, C), F32),
            pltpu.VMEM((2, 8, C), F32),
            pltpu.VMEM((members, 8, C), F32),
            pltpu.VMEM((members, 8, C), F32),
            pltpu.VMEM((members, 8, C), F32),
            pltpu.VMEM((8, C), F32),
            pltpu.VMEM((members, 8, C), F32),
            pltpu.SemaphoreType.DMA((11,)),
            pltpu.SemaphoreType.DMA((4,)),
            pltpu.SemaphoreType.DMA((4,)),
            pltpu.SemaphoreType.DMA,
            pltpu.SemaphoreType.DMA,
            pltpu.SemaphoreType.DMA,
            pltpu.SemaphoreType.DMA,
            pltpu.SemaphoreType.REGULAR,
        ],
        compiler_params=pltpu.CompilerParams(
            collective_id=0, has_side_effects=True, vmem_limit_bytes=60 * 2**20
        ),
    )
    return jax.shard_map(
        call,
        mesh=mesh,
        in_specs=(
            P(None, ("slab", "grp")),
            P(("slab", "grp")),
            P(("slab", "grp"), None),
            P(),
            P(),
            P(),
            P(),
            P(),
            P(),
            P(("slab", "grp"), None),
            P(("slab", "grp")),
        ),
        out_specs=(P(("slab", "grp")), P(None, ("slab", "grp"))),
        check_vma=False,
    )
```

```python
import functools

import jax
import jax.numpy as jnp
from jax import lax
from jax.experimental import pallas as pl
from jax.experimental.pallas import tpu as pltpu
from jax.sharding import PartitionSpec as P

BLOCK = 64
C = 128
ROWS = 72
PAIRS = BLOCK * BLOCK
CHUNK = 512
CENTRES = CHUNK // BLOCK
SPACING = 2.5 / 7
ROWS_OF_PAIRS = PAIRS // 128
ROOT = 1.4426950408889634**0.5
MESH = pl.DeviceIdType.MESH
BF16, F32 = jnp.bfloat16, jnp.float32


def parts(value, count):
    found = []
    for _ in range(count):
        part = value.astype(BF16).astype(F32)
        found.append(part)
        value = value - part
    return found


def dot(left, right):
    return jnp.dot(left, right, preferred_element_type=F32)


def centre_onehot(start, width):
    lane = lax.broadcasted_iota(jnp.int32, (BLOCK, width), 1) + start
    row = lax.broadcasted_iota(jnp.int32, (BLOCK, width), 0)
    return jnp.where((lane // BLOCK) == row, 1.0, 0.0).astype(F32)


def kernel(
    slabs,
    members,
    pos_hbm,
    spc_hbm,
    node_hbm,
    wself_hbm,
    wsend_hbm,
    radial_hbm,
    wmix_hbm,
    readout_hbm,
    scale_hbm,
    nbr_hbm,
    count_hbm,
    energy_ref,
    force_ref,
    pos_ref,
    spc_ref,
    node_ref,
    wself_ref,
    wsend_ref,
    radial_ref,
    wmix_ref,
    readout_ref,
    scale_ref,
    nbr_ref,
    count_ref,
    own,
    near,
    asked,
    centres,
    spread,
    scaled_ref,
    slope_ref,
    energy_rows,
    rhs_pair,
    rhs_centre,
    lhs_send,
    lhs_rest,
    lhs_b,
    lhs_r,
    lhs_m,
    ro_exp,
    pair_acc,
    centre_sums,
    grads,
    near_sum,
    near_grads,
    near_back,
    returned,
    back,
    load_sem,
    send_sem,
    recv_sem,
    own_send_sem,
    own_recv_sem,
    back_send_sem,
    back_recv_sem,
    group_sem,
):
    slab, me = lax.axis_index("slab"), lax.axis_index("grp")
    core = lax.rem(slab, 2)
    sib_slab = slab + 1 - 2 * core
    far_slab = lax.rem(slab - 1 + 2 * core + slabs, slabs)

    barrier = pltpu.get_barrier_semaphore()
    mates = [lax.rem(me + k, members) for k in range(1, members)]
    pl.semaphore_signal(barrier, inc=1, device_id=(far_slab, me), device_id_type=MESH)
    for mate in mates:
        pl.semaphore_signal(
            barrier, inc=1, device_id=(slab + 1 - core, mate), device_id_type=MESH
        )

    @pl.when(core == 0)
    def _():
        pl.semaphore_signal(barrier, inc=1, device_id=(sib_slab, me), device_id_type=MESH)

    loads = [
        pltpu.make_async_copy(source, target, load_sem.at[k])
        for k, (source, target) in enumerate(
            [
                (node_hbm, node_ref),
                (wself_hbm, wself_ref),
                (wsend_hbm, wsend_ref),
                (pos_hbm, pos_ref),
                (spc_hbm, spc_ref),
                (nbr_hbm, nbr_ref),
                (count_hbm, count_ref),
                (radial_hbm, radial_ref),
                (wmix_hbm, wmix_ref),
                (readout_hbm, readout_ref),
                (scale_hbm, scale_ref),
            ]
        )
    ]
    for load in loads:
        load.start()

    for load in loads[:7]:
        load.wait()

    species = spc_ref[...].astype(F32).reshape(1, BLOCK)
    pad = jnp.zeros((1, BLOCK), F32)
    place = jnp.concatenate([pos_ref[...], species, pad, pad, pad, pad], axis=0)
    place = jnp.concatenate([place, jnp.zeros_like(place)], axis=1)
    features = dot(node_ref[...], wself_ref[...])
    own[me, 0:BLOCK, :] = dot(node_ref[...], wsend_ref[...])
    own[me, BLOCK:ROWS, :] = place
    asked_row = lax.broadcasted_iota(jnp.int32, (3 * members, C), 0)

    def slots_in(panel, first):
        hot = jnp.zeros((3 * members, C), F32)
        for k, slot in enumerate((first, 2, 3)):
            other = nbr_ref[0, slot]
            wanted = jnp.where(
                (other // members == panel) & (slot < count_ref[0]),
                lax.rem(other, members) + k * members,
                -1,
            )
            hot = jnp.where(asked_row == wanted, 1.0, hot)
        return hot

    centres[0:BLOCK, :] = features
    centres[BLOCK:ROWS, :] = place
    centres[ROWS:, :] = slots_in(2 * core, core)
    asked[1, 0:BLOCK, :] = features
    asked[1, BLOCK:ROWS, :] = place
    asked[1, ROWS : ROWS + 3 * members, :] = slots_in(1, 1 - core)
    asked[1, ROWS + 3 * members :, :] = slots_in(2 - 2 * core, 1 - core)
    asked[0, ROWS + 3 * members :, :] = jnp.zeros((3 * members, C), F32)

    @pl.when(core == 1)
    def _():
        pl.semaphore_wait(barrier, 2 * members)
        pl.semaphore_signal(group_sem, inc=1, device_id=(sib_slab, me), device_id_type=MESH)

    @pl.when(core == 0)
    def _():
        pl.semaphore_wait(group_sem, 1)

    for mate in mates:
        pltpu.make_async_remote_copy(
            src_ref=own.at[me],
            dst_ref=own.at[me],
            send_sem=own_send_sem,
            recv_sem=own_recv_sem,
            device_id=(slab, mate),
            device_id_type=MESH,
        ).start()

    def copy(index, source, target, to_slab):
        return pltpu.make_async_remote_copy(
            src_ref=source,
            dst_ref=target,
            send_sem=send_sem.at[index],
            recv_sem=recv_sem.at[index],
            device_id=(to_slab, me),
            device_id_type=MESH,
        )

    ask = copy(0, centres, asked.at[0, pl.ds(0, ROWS + 3 * members)], far_slab)
    tell = copy(1, centre_sums.at[0], returned, far_slab)
    lend = copy(2, own, near, sib_slab)
    repay = copy(3, near_grads, near_back, sib_slab)
    early = slab == 0

    def ask_far():
        @pl.when(core == 0)
        def _():
            pl.semaphore_wait(barrier, 1)

        ask.start()

    pl.when(jnp.logical_not(early))(ask_far)

    atom = lax.broadcasted_iota(jnp.int32, (BLOCK, CHUNK), 0)
    lane = lax.broadcasted_iota(jnp.int32, (BLOCK, CHUNK), 1)
    hot_j = jnp.where(lax.rem(lane, BLOCK) == atom, 1.0, 0.0).astype(F32)
    rhs_pair[...] = jnp.concatenate([hot_j, hot_j], axis=0).astype(BF16)
    hot_i = centre_onehot(0, CHUNK)[0:CENTRES]
    rhs_centre[...] = jnp.concatenate([hot_i, hot_i], axis=0).astype(BF16)
    for load in loads[7:]:
        load.wait()
    radial_hi, radial_lo = parts(radial_ref[...], 2)
    lhs_r[...] = (jnp.concatenate([radial_hi, radial_lo], axis=0) * 0.25).astype(BF16)
    lhs_m[...] = (wmix_ref[...].astype(F32).T * 0.5).astype(BF16)
    ones = jnp.ones((16, C), F32)
    lhs_b[...] = jnp.concatenate(
        [
            jnp.concatenate([jnp.zeros((C, C), F32), ones], axis=0),
            jnp.concatenate([wmix_ref[...].astype(F32), jnp.zeros((16, C), F32)], axis=0),
        ],
        axis=1,
    ).astype(BF16)
    readout = readout_ref[...].reshape(1, C)
    ro_exp[...] = jnp.broadcast_to(readout, (C, C)).T
    grads[...] = jnp.zeros_like(grads)
    near_sum[...] = jnp.zeros_like(near_sum)

    row8 = lax.broadcasted_iota(jnp.int32, (8, BLOCK), 0)
    center = lax.broadcasted_iota(jnp.int32, (8, CHUNK), 0).astype(F32) * ROOT
    line = lax.broadcasted_iota(jnp.int32, (ROWS_OF_PAIRS, BLOCK), 0)
    atom = lax.broadcasted_iota(jnp.int32, (ROWS_OF_PAIRS, BLOCK), 1)
    on_line = jnp.where(atom // 2 == line, 1.0, 0.0)
    lane = lax.broadcasted_iota(jnp.int32, (BLOCK, C), 1)
    atom = lax.broadcasted_iota(jnp.int32, (BLOCK, C), 0)
    in_half = jnp.where(lax.rem(atom, 2) == lane // BLOCK, 1.0, 0.0).astype(BF16)
    line = lax.broadcasted_iota(jnp.int32, (ROWS_OF_PAIRS, C), 0)
    lane = lax.broadcasted_iota(jnp.int32, (ROWS_OF_PAIRS, C), 1)
    same_atom = jnp.where(2 * line + lane // BLOCK == lax.rem(lane, BLOCK), 1.0, 0.0)
    mates_blocks = own.at[pl.ds(0, members - 1)]
    mates_grads = grads.at[pl.ds(0, members - 1)]

    pltpu.make_async_copy(mates_blocks, mates_blocks, own_recv_sem).wait()
    lend.start()
    lend.wait_recv()

    def group(turn, carry):
        which = jnp.where(early, 1 - turn, turn)

        @pl.when(which == 0)
        def _():
            ask.wait_recv()

        spot = asked[which, BLOCK:ROWS, 0:BLOCK]
        scale8 = jnp.zeros((8, BLOCK), F32)
        for r in range(4):
            for s in range(4):
                there = (row8 == s) & (spot[3:4] == float(r))
                scale8 = jnp.where(there, scale_ref[r, s], scale8)
        wide = []
        for values in [spot[k : k + 1] for k in range(3)] + [scale8[k : k + 1] for k in range(4)]:
            wide += [on_line * part for part in parts(values, 3)]
        found = dot(jnp.concatenate(wide, axis=0).astype(BF16), in_half)
        for k in range(7):
            base = k * 3 * ROWS_OF_PAIRS
            one, two, three = (
                found[base + p * ROWS_OF_PAIRS : base + (p + 1) * ROWS_OF_PAIRS] for p in range(3)
            )
            spread[k] = one + two + three
        half_hi, half_lo = parts(radial_ref[...] * 0.5, 2)
        for k in range(PAIRS // CHUNK):
            mine = pl.ds(k * CENTRES, CENTRES)
            self_hi, self_lo = parts(asked[which, mine, :] * 0.5, 2)
            rest = [half_hi, half_lo, half_hi, jnp.zeros((8, C), F32), self_hi, self_lo]
            lhs_rest[k] = jnp.concatenate(rest, axis=0).T.astype(BF16)
        pair_acc[...] = jnp.zeros_like(pair_acc)

        @pl.when(early & (which == 1))
        def _():
            ask_far()

        def begin(slot):
            hot_rows = pl.ds(ROWS + slot * members, members)
            near_rows = pl.ds(ROWS + (slot + 3) * members, members)
            hot = asked[which, hot_rows, :]
            near_hot = asked[which, near_rows, :]
            live = jnp.sum(hot + near_hot, axis=0, keepdims=True)
            self_hot = asked[which, pl.ds(ROWS + slot * members + me, 1), :]
            self_hot = jnp.where(which == 1, self_hot, 0.0)
            block = own[0] * hot[0:1] + near[0] * near_hot[0:1]
            for k in range(1, members):
                block = block + own[k] * hot[k : k + 1] + near[k] * near_hot[k : k + 1]
            lhs_send[slot] = jnp.concatenate(parts(block[0:BLOCK] * 0.5, 2), axis=0).T.astype(BF16)
            place_j = block[BLOCK:ROWS, 0:BLOCK]
            place_j = jnp.concatenate([place_j, place_j], axis=1)
            diff = [place_j[k : k + 1] - spread[k] for k in range(3)]
            dist_sq = diff[0] * diff[0] + diff[1] * diff[1] + diff[2] * diff[2]
            kind = place_j[3:4]
            scale = jnp.where(
                kind == 0.0,
                spread[3],
                jnp.where(kind == 1.0, spread[4], jnp.where(kind == 2.0, spread[5], spread[6])),
            )
            scaled = dist_sq * scale
            scaled_ref[slot] = scaled * (ROOT / SPACING)
            keep = live - self_hot * same_atom
            reach = jnp.maximum(1.0 - scaled * (1.0 / 2.5), 0.0)
            return hot, near_hot, diff, scale, keep, reach

        def first(slot, turn):
            base = turn * (CHUNK // C)
            wide = [scaled_ref[slot, base + k : base + k + 1, :] for k in range(CHUNK // C)]
            offset = jnp.concatenate(wide, axis=1) - center
            basis = jnp.exp2(-(offset * offset))
            slope = basis * offset
            basis_hi, basis_lo = parts(basis, 2)
            head = jnp.concatenate(
                [basis_hi, basis_hi, basis_lo, jnp.zeros((8, CHUNK), F32)], axis=0
            ).astype(BF16)
            rhs = jnp.concatenate([rhs_pair[...], head, rhs_centre[...]], axis=0)
            lhs = jnp.concatenate([lhs_send[slot], lhs_rest[turn]], axis=1)
            return slot, base, slope, dot(lhs, rhs)

        def second(state):
            half = state[-1]
            t = jnp.tanh(half)
            p = 1.0 + t
            hidden = half * p
            slope_1 = p + hidden * (1.0 - t)
            half = dot(lhs_m[...], hidden.astype(BF16))
            return state[:-1] + (slope_1, half)

        def third(state):
            half = state[-1]
            t = jnp.tanh(half)
            p = (1.0 + t) * jnp.concatenate([ro_exp[...]] * (CHUNK // C), axis=1)
            mixed = half * p
            mixed = mixed.astype(BF16)
            slope_2 = p.astype(BF16) + mixed * (1.0 - t.astype(BF16))
            out = dot(lhs_b[...], jnp.concatenate([mixed, slope_2], axis=0))
            return state[:-1] + (out,)

        def fourth(state):
            slot, base, slope, slope_1, out = state
            d_basis = dot(lhs_r[...], (out[0:C] * slope_1).astype(BF16))
            slope = jnp.sum((d_basis[0:8] + d_basis[8:16]) * slope, axis=0, keepdims=True)
            for k in range(CHUNK // C):
                lanes = slice(k * C, (k + 1) * C)
                slope_ref[slot, base + k : base + k + 1, :] = slope[:, lanes]
                energy_rows[slot, base + k : base + k + 1, :] = out[C : C + 1, lanes]

        def finish(slot, known):
            hot, near_hot, diff, scale, keep, reach = known
            energy = energy_rows[slot]
            cut = reach * reach
            d_scaled = cut * slope_ref[slot] * (-2.0 / (SPACING * ROOT))
            d_scaled = 2.0 * keep * scale * (d_scaled - (2.0 / 2.5) * reach * energy)
            found = [d_scaled * part for part in diff]
            for k in range(3):
                pair_acc[k] += found[k]
            pair_acc[3] += keep * cut * energy
            total = [jnp.sum(part, axis=0, keepdims=True) for part in found]
            total = jnp.concatenate(total + [jnp.zeros((5, C), F32)], axis=0)
            grad = total[:, 0:BLOCK] + total[:, BLOCK:C]
            grad = jnp.concatenate([grad, jnp.zeros_like(grad)], axis=1)
            for k in range(members):
                grads[k] += grad * hot[k : k + 1]
                near_sum[k] += grad * near_hot[k : k + 1]

        stages = [first, second, third, fourth]
        count = PAIRS // CHUNK
        known, states = {}, {}
        for turn in range(3 * count + 3):
            for depth in range(4):
                sub = turn - depth
                if not 0 <= sub < 3 * count:
                    continue
                slot, part = divmod(sub, count)
                if depth == 0:
                    if sub == 0:
                        known[0] = begin(0)
                    if part == count - 1 and slot < 2:
                        known[slot + 1] = begin(slot + 1)
                    states[sub] = first(slot, part)
                else:
                    states[sub] = stages[depth](states[sub])
                if depth == 3 and part == count - 1:
                    finish(slot, known.pop(slot))

        wide = []
        for k in range(4):
            wide += parts(pair_acc[k], 3)
        found = lax.dot_general(
            jnp.concatenate(wide, axis=0).astype(BF16),
            in_half,
            (((1,), (1,)), ((), ())),
            preferred_element_type=F32,
        )
        total = []
        for k in range(4):
            base = k * 3 * ROWS_OF_PAIRS
            one, two, three = (
                found[base + p * ROWS_OF_PAIRS : base + (p + 1) * ROWS_OF_PAIRS] for p in range(3)
            )
            total.append(jnp.sum((one + two + three) * on_line, axis=0, keepdims=True))
        total = jnp.concatenate(total + [jnp.zeros((4, BLOCK), F32)], axis=0)
        centre_sums[which] = jnp.concatenate([total, jnp.zeros_like(total)], axis=1)

        @pl.when(which == 0)
        def _():
            tell.start()

        @pl.when(which == 1)
        def _():
            near_grads[...] = near_sum[...]
            repay.start()

        return carry

    lax.fori_loop(0, 2, group, 0)

    repay.wait_recv()
    grads[...] += near_back[...]
    for mate in mates:
        pltpu.make_async_remote_copy(
            src_ref=grads.at[mate],
            dst_ref=back.at[me],
            send_sem=back_send_sem,
            recv_sem=back_recv_sem,
            device_id=(slab, mate),
            device_id_type=MESH,
        ).start()
    back[me] = grads[me]

    tell.wait_recv()
    centre_sum = centre_sums[1] + returned[...]
    energy_ref[...] = centre_sum[3:4, 0:BLOCK].reshape(BLOCK)
    pltpu.make_async_copy(mates_grads, mates_grads, back_recv_sem).wait()
    total = back[0]
    for k in range(1, members):
        total = total + back[k]
    force_ref[...] = (centre_sum - total)[0:3, 0:BLOCK]

    for sent in (ask, tell, lend, repay):
        sent.wait_send()
    pltpu.make_async_copy(mates_blocks, mates_blocks, own_send_sem).wait()
    pltpu.make_async_copy(mates_grads, mates_grads, back_send_sem).wait()


def solution(mesh):
    slabs, members = mesh.shape["slab"], mesh.shape["grp"]
    vmem = pl.BlockSpec(memory_space=pltpu.VMEM)
    call = pl.pallas_call(
        functools.partial(kernel, slabs, members),
        out_shape=(
            jax.ShapeDtypeStruct((BLOCK,), F32),
            jax.ShapeDtypeStruct((3, BLOCK), F32),
        ),
        in_specs=[pl.BlockSpec(memory_space=pltpu.HBM)] * 11,
        out_specs=(vmem, vmem),
        scratch_shapes=[
            pltpu.VMEM((3, BLOCK), F32),
            pltpu.VMEM((BLOCK,), jnp.int32),
            pltpu.VMEM((BLOCK, C), BF16),
            pltpu.VMEM((C, C), BF16),
            pltpu.VMEM((C, C), BF16),
            pltpu.VMEM((8, C), F32),
            pltpu.VMEM((C, C), BF16),
            pltpu.VMEM((C,), F32),
            pltpu.SMEM((4, 4), F32),
            pltpu.SMEM((1, 4), jnp.int32),
            pltpu.SMEM((1,), jnp.int32),
            pltpu.VMEM((members, ROWS, C), F32),
            pltpu.VMEM((members, ROWS, C), F32),
            pltpu.VMEM((2, ROWS + 6 * members, C), F32),
            pltpu.VMEM((ROWS + 3 * members, C), F32),
            pltpu.VMEM((7, ROWS_OF_PAIRS, C), F32),
            pltpu.VMEM((3, ROWS_OF_PAIRS, C), F32),
            pltpu.VMEM((3, ROWS_OF_PAIRS, C), F32),
            pltpu.VMEM((3, ROWS_OF_PAIRS, C), F32),
            pltpu.VMEM((2 * BLOCK, CHUNK), BF16),
            pltpu.VMEM((2 * CENTRES, CHUNK), BF16),
            pltpu.VMEM((3, C, 2 * BLOCK), BF16),
            pltpu.VMEM((PAIRS // CHUNK, C, 32 + 2 * CENTRES), BF16),
            pltpu.VMEM((C + 16, 2 * C), BF16),
            pltpu.VMEM((16, C), BF16),
            pltpu.VMEM((C, C), BF16),
            pltpu.VMEM((C, C), F32),
            pltpu.VMEM((4, ROWS_OF_PAIRS, C), F32),
            pltpu.VMEM((2, 8, C), F32),
            pltpu.VMEM((members, 8, C), F32),
            pltpu.VMEM((members, 8, C), F32),
            pltpu.VMEM((members, 8, C), F32),
            pltpu.VMEM((members, 8, C), F32),
            pltpu.VMEM((8, C), F32),
            pltpu.VMEM((members, 8, C), F32),
            pltpu.SemaphoreType.DMA((11,)),
            pltpu.SemaphoreType.DMA((4,)),
            pltpu.SemaphoreType.DMA((4,)),
            pltpu.SemaphoreType.DMA,
            pltpu.SemaphoreType.DMA,
            pltpu.SemaphoreType.DMA,
            pltpu.SemaphoreType.DMA,
            pltpu.SemaphoreType.REGULAR,
        ],
        compiler_params=pltpu.CompilerParams(
            collective_id=0, has_side_effects=True, vmem_limit_bytes=60 * 2**20
        ),
    )
    return jax.shard_map(
        call,
        mesh=mesh,
        in_specs=(
            P(None, ("slab", "grp")),
            P(("slab", "grp")),
            P(("slab", "grp"), None),
            P(),
            P(),
            P(),
            P(),
            P(),
            P(),
            P(("slab", "grp"), None),
            P(("slab", "grp")),
        ),
        out_specs=(P(("slab", "grp")), P(None, ("slab", "grp"))),
        check_vma=False,
    )
```

```python
import functools

import jax
import jax.numpy as jnp
from jax import lax
from jax.experimental import pallas as pl
from jax.experimental.pallas import tpu as pltpu
from jax.sharding import PartitionSpec as P

BLOCK = 64
C = 128
ROWS = 72
PAIRS = BLOCK * BLOCK
CHUNK = 512
CENTRES = CHUNK // BLOCK
SPACING = 2.5 / 7
ROWS_OF_PAIRS = PAIRS // 128
ROOT = 1.4426950408889634**0.5
MESH = pl.DeviceIdType.MESH
BF16, F32 = jnp.bfloat16, jnp.float32


def parts(value, count):
    found = []
    for _ in range(count):
        part = value.astype(BF16).astype(F32)
        found.append(part)
        value = value - part
    return found


def dot(left, right):
    return jnp.dot(left, right, preferred_element_type=F32)


def centre_onehot(start, width):
    lane = lax.broadcasted_iota(jnp.int32, (BLOCK, width), 1) + start
    row = lax.broadcasted_iota(jnp.int32, (BLOCK, width), 0)
    return jnp.where((lane // BLOCK) == row, 1.0, 0.0).astype(F32)


def kernel(
    slabs,
    members,
    pos_hbm,
    spc_hbm,
    node_hbm,
    wself_hbm,
    wsend_hbm,
    radial_hbm,
    wmix_hbm,
    readout_hbm,
    scale_hbm,
    nbr_hbm,
    count_hbm,
    energy_ref,
    force_ref,
    pos_ref,
    spc_ref,
    node_ref,
    wself_ref,
    wsend_ref,
    radial_ref,
    wmix_ref,
    readout_ref,
    scale_ref,
    nbr_ref,
    count_ref,
    own,
    near,
    near_used,
    asked,
    centres,
    spread,
    scaled_ref,
    slope_ref,
    energy_rows,
    rhs_pair,
    rhs_centre,
    lhs_send,
    lhs_rest,
    lhs_b,
    lhs_r,
    lhs_m,
    ro_exp,
    pair_acc,
    centre_sums,
    grads,
    near_sum,
    near_grads,
    near_back,
    returned,
    back,
    load_sem,
    send_sem,
    recv_sem,
    own_send_sem,
    own_recv_sem,
    near_send_sem,
    near_recv_sem,
    back_send_sem,
    back_recv_sem,
    group_sem,
):
    slab, me = lax.axis_index("slab"), lax.axis_index("grp")
    core = lax.rem(slab, 2)
    sib_slab = slab + 1 - 2 * core
    far_slab = lax.rem(slab - 1 + 2 * core + slabs, slabs)

    barrier = pltpu.get_barrier_semaphore()
    mates = [lax.rem(me + k, members) for k in range(1, members)]
    pl.semaphore_signal(barrier, inc=1, device_id=(far_slab, me), device_id_type=MESH)
    for mate in mates:
        pl.semaphore_signal(
            barrier, inc=1, device_id=(slab + 1 - core, mate), device_id_type=MESH
        )

    @pl.when(core == 0)
    def _():
        pl.semaphore_signal(barrier, inc=1, device_id=(sib_slab, me), device_id_type=MESH)

    loads = [
        pltpu.make_async_copy(source, target, load_sem.at[k])
        for k, (source, target) in enumerate(
            [
                (node_hbm, node_ref),
                (wself_hbm, wself_ref),
                (wsend_hbm, wsend_ref),
                (pos_hbm, pos_ref),
                (spc_hbm, spc_ref),
                (nbr_hbm, nbr_ref),
                (count_hbm, count_ref),
                (radial_hbm, radial_ref),
                (wmix_hbm, wmix_ref),
                (readout_hbm, readout_ref),
                (scale_hbm, scale_ref),
            ]
        )
    ]
    for load in loads:
        load.start()

    for load in loads[:7]:
        load.wait()

    species = spc_ref[...].astype(F32).reshape(1, BLOCK)
    pad = jnp.zeros((1, BLOCK), F32)
    place = jnp.concatenate([pos_ref[...], species, pad, pad, pad, pad], axis=0)
    place = jnp.concatenate([place, jnp.zeros_like(place)], axis=1)
    features = dot(node_ref[...], wself_ref[...])
    own[me, 0:BLOCK, :] = dot(node_ref[...], wsend_ref[...])
    own[me, BLOCK:ROWS, :] = place
    asked_row = lax.broadcasted_iota(jnp.int32, (3 * members, C), 0)

    def slots_in(panel, first):
        hot = jnp.zeros((3 * members, C), F32)
        for k, slot in enumerate((first, 2, 3)):
            other = nbr_ref[0, slot]
            wanted = jnp.where(
                (other // members == panel) & (slot < count_ref[0]),
                lax.rem(other, members) + k * members,
                -1,
            )
            hot = jnp.where(asked_row == wanted, 1.0, hot)
        return hot

    centres[0:BLOCK, :] = features
    centres[BLOCK:ROWS, :] = place
    centres[ROWS:, :] = slots_in(2 * core, core)
    asked[1, 0:BLOCK, :] = features
    asked[1, BLOCK:ROWS, :] = place
    asked[1, ROWS : ROWS + 3 * members, :] = slots_in(1, 1 - core)
    asked[1, ROWS + 3 * members :, :] = slots_in(2 - 2 * core, 1 - core)
    asked[0, ROWS + 3 * members :, :] = jnp.zeros((3 * members, C), F32)

    @pl.when(core == 1)
    def _():
        pl.semaphore_wait(barrier, 2 * members)
        pl.semaphore_signal(group_sem, inc=1, device_id=(sib_slab, me), device_id_type=MESH)

    @pl.when(core == 0)
    def _():
        pl.semaphore_wait(group_sem, 1)

    def arrival(member, to=me):
        return pltpu.make_async_remote_copy(
            src_ref=own.at[member],
            dst_ref=own.at[member],
            send_sem=own_send_sem,
            recv_sem=own_recv_sem.at[member],
            device_id=(slab, to),
            device_id_type=MESH,
        )

    def lend(member):
        return pltpu.make_async_remote_copy(
            src_ref=own.at[member],
            dst_ref=near.at[member],
            send_sem=near_send_sem,
            recv_sem=near_recv_sem.at[member],
            device_id=(sib_slab, me),
            device_id_type=MESH,
        )

    for mate in mates:
        arrival(me, mate).start()
    lend(me).start()

    def copy(index, source, target, to_slab):
        return pltpu.make_async_remote_copy(
            src_ref=source,
            dst_ref=target,
            send_sem=send_sem.at[index],
            recv_sem=recv_sem.at[index],
            device_id=(to_slab, me),
            device_id_type=MESH,
        )

    ask = copy(0, centres, asked.at[0, pl.ds(0, ROWS + 3 * members)], far_slab)
    tell = copy(1, centre_sums.at[0], returned, far_slab)
    repay = copy(2, near_grads, near_back, sib_slab)
    early = slab == 0

    def ask_far():
        @pl.when(core == 0)
        def _():
            pl.semaphore_wait(barrier, 1)

        ask.start()

    pl.when(jnp.logical_not(early))(ask_far)

    atom = lax.broadcasted_iota(jnp.int32, (BLOCK, CHUNK), 0)
    lane = lax.broadcasted_iota(jnp.int32, (BLOCK, CHUNK), 1)
    hot_j = jnp.where(lax.rem(lane, BLOCK) == atom, 1.0, 0.0).astype(F32)
    rhs_pair[...] = jnp.concatenate([hot_j, hot_j], axis=0).astype(BF16)
    hot_i = centre_onehot(0, CHUNK)[0:CENTRES]
    rhs_centre[...] = jnp.concatenate([hot_i, hot_i], axis=0).astype(BF16)
    for load in loads[7:]:
        load.wait()
    radial_hi, radial_lo = parts(radial_ref[...], 2)
    lhs_r[...] = (jnp.concatenate([radial_hi, radial_lo], axis=0) * 0.25).astype(BF16)
    lhs_m[...] = (wmix_ref[...].astype(F32).T * 0.5).astype(BF16)
    ones = jnp.ones((16, C), F32)
    lhs_b[...] = jnp.concatenate(
        [
            jnp.concatenate([jnp.zeros((C, C), F32), ones], axis=0),
            jnp.concatenate([wmix_ref[...].astype(F32), jnp.zeros((16, C), F32)], axis=0),
        ],
        axis=1,
    ).astype(BF16)
    readout = readout_ref[...].reshape(1, C)
    ro_exp[...] = jnp.broadcast_to(readout, (C, C)).T
    grads[...] = jnp.zeros_like(grads)
    near_sum[...] = jnp.zeros_like(near_sum)

    row8 = lax.broadcasted_iota(jnp.int32, (8, BLOCK), 0)
    center = lax.broadcasted_iota(jnp.int32, (8, CHUNK), 0).astype(F32) * ROOT
    line = lax.broadcasted_iota(jnp.int32, (ROWS_OF_PAIRS, BLOCK), 0)
    atom = lax.broadcasted_iota(jnp.int32, (ROWS_OF_PAIRS, BLOCK), 1)
    on_line = jnp.where(atom // 2 == line, 1.0, 0.0)
    lane = lax.broadcasted_iota(jnp.int32, (BLOCK, C), 1)
    atom = lax.broadcasted_iota(jnp.int32, (BLOCK, C), 0)
    in_half = jnp.where(lax.rem(atom, 2) == lane // BLOCK, 1.0, 0.0).astype(BF16)
    line = lax.broadcasted_iota(jnp.int32, (ROWS_OF_PAIRS, C), 0)
    lane = lax.broadcasted_iota(jnp.int32, (ROWS_OF_PAIRS, C), 1)
    same_atom = jnp.where(2 * line + lane // BLOCK == lax.rem(lane, BLOCK), 1.0, 0.0)
    mates_blocks = own.at[pl.ds(0, members - 1)]
    mates_grads = grads.at[pl.ds(0, members - 1)]

    for mate in mates:
        arrival(mate).wait_recv()
        lend(mate).start()
    pl.when(early)(ask_far)

    def group(turn, carry):
        which = jnp.where(early, 1 - turn, turn)

        @pl.when(which == 0)
        def _():
            ask.wait_recv()
            near_used[...] = jnp.zeros_like(near_used)

        @pl.when(which == 1)
        def _():
            for block in range(members):
                lend(block).wait_recv()
            near_used[...] = near[...]

        spot = asked[which, BLOCK:ROWS, 0:BLOCK]
        scale8 = jnp.zeros((8, BLOCK), F32)
        for r in range(4):
            for s in range(4):
                there = (row8 == s) & (spot[3:4] == float(r))
                scale8 = jnp.where(there, scale_ref[r, s], scale8)
        wide = []
        for values in [spot[k : k + 1] for k in range(3)] + [scale8[k : k + 1] for k in range(4)]:
            wide += [on_line * part for part in parts(values, 3)]
        found = dot(jnp.concatenate(wide, axis=0).astype(BF16), in_half)
        for k in range(7):
            base = k * 3 * ROWS_OF_PAIRS
            one, two, three = (
                found[base + p * ROWS_OF_PAIRS : base + (p + 1) * ROWS_OF_PAIRS] for p in range(3)
            )
            spread[k] = one + two + three
        half_hi, half_lo = parts(radial_ref[...] * 0.5, 2)
        for k in range(PAIRS // CHUNK):
            mine = pl.ds(k * CENTRES, CENTRES)
            self_hi, self_lo = parts(asked[which, mine, :] * 0.5, 2)
            rest = [half_hi, half_lo, half_hi, jnp.zeros((8, C), F32), self_hi, self_lo]
            lhs_rest[k] = jnp.concatenate(rest, axis=0).T.astype(BF16)
        pair_acc[...] = jnp.zeros_like(pair_acc)

        def begin(slot):
            hot_rows = pl.ds(ROWS + slot * members, members)
            near_rows = pl.ds(ROWS + (slot + 3) * members, members)
            hot = asked[which, hot_rows, :]
            near_hot = asked[which, near_rows, :]
            live = jnp.sum(hot + near_hot, axis=0, keepdims=True)
            self_hot = asked[which, pl.ds(ROWS + slot * members + me, 1), :]
            self_hot = jnp.where(which == 1, self_hot, 0.0)
            block = own[0] * hot[0:1] + near_used[0] * near_hot[0:1]
            for k in range(1, members):
                block = block + own[k] * hot[k : k + 1] + near_used[k] * near_hot[k : k + 1]
            lhs_send[slot] = jnp.concatenate(parts(block[0:BLOCK] * 0.5, 2), axis=0).T.astype(BF16)
            place_j = block[BLOCK:ROWS, 0:BLOCK]
            place_j = jnp.concatenate([place_j, place_j], axis=1)
            diff = [place_j[k : k + 1] - spread[k] for k in range(3)]
            dist_sq = diff[0] * diff[0] + diff[1] * diff[1] + diff[2] * diff[2]
            kind = place_j[3:4]
            scale = jnp.where(
                kind == 0.0,
                spread[3],
                jnp.where(kind == 1.0, spread[4], jnp.where(kind == 2.0, spread[5], spread[6])),
            )
            scaled = dist_sq * scale
            scaled_ref[slot] = scaled * (ROOT / SPACING)
            keep = live - self_hot * same_atom
            reach = jnp.maximum(1.0 - scaled * (1.0 / 2.5), 0.0)
            return hot, near_hot, diff, scale, keep, reach

        def first(slot, turn):
            base = turn * (CHUNK // C)
            wide = [scaled_ref[slot, base + k : base + k + 1, :] for k in range(CHUNK // C)]
            offset = jnp.concatenate(wide, axis=1) - center
            basis = jnp.exp2(-(offset * offset))
            slope = basis * offset
            basis_hi, basis_lo = parts(basis, 2)
            head = jnp.concatenate(
                [basis_hi, basis_hi, basis_lo, jnp.zeros((8, CHUNK), F32)], axis=0
            ).astype(BF16)
            rhs = jnp.concatenate([rhs_pair[...], head, rhs_centre[...]], axis=0)
            lhs = jnp.concatenate([lhs_send[slot], lhs_rest[turn]], axis=1)
            return slot, base, slope, dot(lhs, rhs)

        def second(state):
            half = state[-1]
            t = jnp.tanh(half)
            p = 1.0 + t
            hidden = (half * p).astype(BF16)
            t = t.astype(BF16)
            slope_1 = (1.0 + t) + hidden * (1.0 - t)
            half = dot(lhs_m[...], hidden)
            return state[:-1] + (slope_1, half)

        def third(state):
            half = state[-1]
            t = jnp.tanh(half)
            p = (1.0 + t) * jnp.concatenate([ro_exp[...]] * (CHUNK // C), axis=1)
            mixed = half * p
            mixed = mixed.astype(BF16)
            slope_2 = p.astype(BF16) + mixed * (1.0 - t.astype(BF16))
            out = dot(lhs_b[...], jnp.concatenate([mixed, slope_2], axis=0))
            return state[:-1] + (out,)

        def fourth(state):
            slot, base, slope, slope_1, out = state
            d_basis = dot(lhs_r[...], out[0:C].astype(BF16) * slope_1)
            slope = jnp.sum((d_basis[0:8] + d_basis[8:16]) * slope, axis=0, keepdims=True)
            for k in range(CHUNK // C):
                lanes = slice(k * C, (k + 1) * C)
                slope_ref[slot, base + k : base + k + 1, :] = slope[:, lanes]
                energy_rows[slot, base + k : base + k + 1, :] = out[C : C + 1, lanes]

        def finish(slot, known):
            hot, near_hot, diff, scale, keep, reach = known
            energy = energy_rows[slot]
            cut = reach * reach
            d_scaled = cut * slope_ref[slot] * (-2.0 / (SPACING * ROOT))
            d_scaled = 2.0 * keep * scale * (d_scaled - (2.0 / 2.5) * reach * energy)
            found = [d_scaled * part for part in diff]
            for k in range(3):
                pair_acc[k] += found[k]
            pair_acc[3] += keep * cut * energy
            total = [jnp.sum(part, axis=0, keepdims=True) for part in found]
            total = jnp.concatenate(total + [jnp.zeros((5, C), F32)], axis=0)
            grad = total[:, 0:BLOCK] + total[:, BLOCK:C]
            grad = jnp.concatenate([grad, jnp.zeros_like(grad)], axis=1)
            for k in range(members):
                grads[k] += grad * hot[k : k + 1]
                near_sum[k] += grad * near_hot[k : k + 1]

        stages = [first, second, third, fourth]
        count = PAIRS // CHUNK
        known, states = {}, {}
        for turn in range(3 * count + 3):
            for depth in range(4):
                sub = turn - depth
                if not 0 <= sub < 3 * count:
                    continue
                slot, part = divmod(sub, count)
                if depth == 0:
                    if sub == 0:
                        known[0] = begin(0)
                    if part == count - 1 and slot < 2:
                        known[slot + 1] = begin(slot + 1)
                    states[sub] = first(slot, part)
                else:
                    states[sub] = stages[depth](states[sub])
                if depth == 3 and part == count - 1:
                    finish(slot, known.pop(slot))

        wide = []
        for k in range(4):
            wide += parts(pair_acc[k], 3)
        found = lax.dot_general(
            jnp.concatenate(wide, axis=0).astype(BF16),
            in_half,
            (((1,), (1,)), ((), ())),
            preferred_element_type=F32,
        )
        total = []
        for k in range(4):
            base = k * 3 * ROWS_OF_PAIRS
            one, two, three = (
                found[base + p * ROWS_OF_PAIRS : base + (p + 1) * ROWS_OF_PAIRS] for p in range(3)
            )
            total.append(jnp.sum((one + two + three) * on_line, axis=0, keepdims=True))
        total = jnp.concatenate(total + [jnp.zeros((4, BLOCK), F32)], axis=0)
        centre_sums[which] = jnp.concatenate([total, jnp.zeros_like(total)], axis=1)

        @pl.when(which == 0)
        def _():
            tell.start()

        @pl.when(which == 1)
        def _():
            near_grads[...] = near_sum[...]
            repay.start()

        return carry

    lax.fori_loop(0, 2, group, 0)

    repay.wait_recv()
    grads[...] += near_back[...]
    for mate in mates:
        pltpu.make_async_remote_copy(
            src_ref=grads.at[mate],
            dst_ref=back.at[me],
            send_sem=back_send_sem,
            recv_sem=back_recv_sem,
            device_id=(slab, mate),
            device_id_type=MESH,
        ).start()
    back[me] = grads[me]

    tell.wait_recv()
    centre_sum = centre_sums[1] + returned[...]
    energy_ref[...] = centre_sum[3:4, 0:BLOCK].reshape(BLOCK)
    pltpu.make_async_copy(mates_grads, mates_grads, back_recv_sem).wait()
    total = back[0]
    for k in range(1, members):
        total = total + back[k]
    force_ref[...] = (centre_sum - total)[0:3, 0:BLOCK]

    for sent in (ask, tell, repay):
        sent.wait_send()
    pltpu.make_async_copy(near, near, near_send_sem).wait()
    pltpu.make_async_copy(mates_blocks, mates_blocks, own_send_sem).wait()
    pltpu.make_async_copy(mates_grads, mates_grads, back_send_sem).wait()


def solution(mesh):
    slabs, members = mesh.shape["slab"], mesh.shape["grp"]
    vmem = pl.BlockSpec(memory_space=pltpu.VMEM)
    call = pl.pallas_call(
        functools.partial(kernel, slabs, members),
        out_shape=(
            jax.ShapeDtypeStruct((BLOCK,), F32),
            jax.ShapeDtypeStruct((3, BLOCK), F32),
        ),
        in_specs=[pl.BlockSpec(memory_space=pltpu.HBM)] * 11,
        out_specs=(vmem, vmem),
        scratch_shapes=[
            pltpu.VMEM((3, BLOCK), F32),
            pltpu.VMEM((BLOCK,), jnp.int32),
            pltpu.VMEM((BLOCK, C), BF16),
            pltpu.VMEM((C, C), BF16),
            pltpu.VMEM((C, C), BF16),
            pltpu.VMEM((8, C), F32),
            pltpu.VMEM((C, C), BF16),
            pltpu.VMEM((C,), F32),
            pltpu.SMEM((4, 4), F32),
            pltpu.SMEM((1, 4), jnp.int32),
            pltpu.SMEM((1,), jnp.int32),
            pltpu.VMEM((members, ROWS, C), F32),
            pltpu.VMEM((members, ROWS, C), F32),
            pltpu.VMEM((members, ROWS, C), F32),
            pltpu.VMEM((2, ROWS + 6 * members, C), F32),
            pltpu.VMEM((ROWS + 3 * members, C), F32),
            pltpu.VMEM((7, ROWS_OF_PAIRS, C), F32),
            pltpu.VMEM((3, ROWS_OF_PAIRS, C), F32),
            pltpu.VMEM((3, ROWS_OF_PAIRS, C), F32),
            pltpu.VMEM((3, ROWS_OF_PAIRS, C), F32),
            pltpu.VMEM((2 * BLOCK, CHUNK), BF16),
            pltpu.VMEM((2 * CENTRES, CHUNK), BF16),
            pltpu.VMEM((3, C, 2 * BLOCK), BF16),
            pltpu.VMEM((PAIRS // CHUNK, C, 32 + 2 * CENTRES), BF16),
            pltpu.VMEM((C + 16, 2 * C), BF16),
            pltpu.VMEM((16, C), BF16),
            pltpu.VMEM((C, C), BF16),
            pltpu.VMEM((C, C), F32),
            pltpu.VMEM((4, ROWS_OF_PAIRS, C), F32),
            pltpu.VMEM((2, 8, C), F32),
            pltpu.VMEM((members, 8, C), F32),
            pltpu.VMEM((members, 8, C), F32),
            pltpu.VMEM((members, 8, C), F32),
            pltpu.VMEM((members, 8, C), F32),
            pltpu.VMEM((8, C), F32),
            pltpu.VMEM((members, 8, C), F32),
            pltpu.SemaphoreType.DMA((11,)),
            pltpu.SemaphoreType.DMA((3,)),
            pltpu.SemaphoreType.DMA((3,)),
            pltpu.SemaphoreType.DMA,
            pltpu.SemaphoreType.DMA((members,)),
            pltpu.SemaphoreType.DMA,
            pltpu.SemaphoreType.DMA((members,)),
            pltpu.SemaphoreType.DMA,
            pltpu.SemaphoreType.DMA,
            pltpu.SemaphoreType.REGULAR,
        ],
        compiler_params=pltpu.CompilerParams(
            collective_id=0, has_side_effects=True, vmem_limit_bytes=60 * 2**20
        ),
    )
    return jax.shard_map(
        call,
        mesh=mesh,
        in_specs=(
            P(None, ("slab", "grp")),
            P(("slab", "grp")),
            P(("slab", "grp"), None),
            P(),
            P(),
            P(),
            P(),
            P(),
            P(),
            P(("slab", "grp"), None),
            P(("slab", "grp")),
        ),
        out_specs=(P(("slab", "grp")), P(None, ("slab", "grp"))),
        check_vma=False,
    )
```

```python
import functools

import jax
import jax.numpy as jnp
from jax import lax
from jax.experimental import pallas as pl
from jax.experimental.pallas import tpu as pltpu
from jax.sharding import PartitionSpec as P

BLOCK = 64
C = 128
ROWS = 72
PAIRS = BLOCK * BLOCK
CHUNK = 512
CENTRES = CHUNK // BLOCK
SPACING = 2.5 / 7
ROWS_OF_PAIRS = PAIRS // 128
ROOT = 1.4426950408889634**0.5
MESH = pl.DeviceIdType.MESH
BF16, F32 = jnp.bfloat16, jnp.float32


def parts(value, count):
    found = []
    for _ in range(count):
        part = value.astype(BF16).astype(F32)
        found.append(part)
        value = value - part
    return found


def dot(left, right):
    return jnp.dot(left, right, preferred_element_type=F32)


def centre_onehot(start, width):
    lane = lax.broadcasted_iota(jnp.int32, (BLOCK, width), 1) + start
    row = lax.broadcasted_iota(jnp.int32, (BLOCK, width), 0)
    return jnp.where((lane // BLOCK) == row, 1.0, 0.0).astype(F32)


def kernel(
    slabs,
    members,
    pos_hbm,
    spc_hbm,
    node_hbm,
    wself_hbm,
    wsend_hbm,
    radial_hbm,
    wmix_hbm,
    readout_hbm,
    scale_hbm,
    nbr_hbm,
    count_hbm,
    energy_ref,
    force_ref,
    pos_ref,
    spc_ref,
    node_ref,
    wself_ref,
    wsend_ref,
    radial_ref,
    wmix_ref,
    readout_ref,
    scale_ref,
    nbr_ref,
    count_ref,
    own,
    near,
    near_used,
    asked,
    centres,
    spread,
    scaled_ref,
    slope_ref,
    energy_rows,
    rhs_pair,
    rhs_centre,
    lhs_send,
    lhs_rest,
    lhs_b,
    lhs_r,
    lhs_m,
    ro_exp,
    pair_acc,
    centre_sums,
    grads,
    near_sum,
    near_grads,
    near_back,
    returned,
    back,
    load_sem,
    send_sem,
    recv_sem,
    own_send_sem,
    own_recv_sem,
    near_send_sem,
    near_recv_sem,
    back_send_sem,
    back_recv_sem,
    group_sem,
):
    slab, me = lax.axis_index("slab"), lax.axis_index("grp")
    core = lax.rem(slab, 2)
    sib_slab = slab + 1 - 2 * core
    far_slab = lax.rem(slab - 1 + 2 * core + slabs, slabs)

    barrier = pltpu.get_barrier_semaphore()
    mates = [lax.rem(me + k, members) for k in range(1, members)]
    pl.semaphore_signal(barrier, inc=1, device_id=(far_slab, me), device_id_type=MESH)
    for mate in mates:
        pl.semaphore_signal(
            barrier, inc=1, device_id=(slab + 1 - core, mate), device_id_type=MESH
        )

    @pl.when(core == 0)
    def _():
        pl.semaphore_signal(barrier, inc=1, device_id=(sib_slab, me), device_id_type=MESH)

    loads = [
        pltpu.make_async_copy(source, target, load_sem.at[k])
        for k, (source, target) in enumerate(
            [
                (node_hbm, node_ref),
                (wself_hbm, wself_ref),
                (wsend_hbm, wsend_ref),
                (pos_hbm, pos_ref),
                (spc_hbm, spc_ref),
                (nbr_hbm, nbr_ref),
                (count_hbm, count_ref),
                (radial_hbm, radial_ref),
                (wmix_hbm, wmix_ref),
                (readout_hbm, readout_ref),
                (scale_hbm, scale_ref),
            ]
        )
    ]
    for load in loads:
        load.start()

    for load in loads[:7]:
        load.wait()

    species = spc_ref[...].astype(F32).reshape(1, BLOCK)
    pad = jnp.zeros((1, BLOCK), F32)
    place = jnp.concatenate([pos_ref[...], species, pad, pad, pad, pad], axis=0)
    place = jnp.concatenate([place, jnp.zeros_like(place)], axis=1)
    features = dot(node_ref[...], wself_ref[...])
    own[me, 0:BLOCK, :] = dot(node_ref[...], wsend_ref[...])
    own[me, BLOCK:ROWS, :] = place
    asked_row = lax.broadcasted_iota(jnp.int32, (3 * members, C), 0)

    def slots_in(panel, first):
        hot = jnp.zeros((3 * members, C), F32)
        for k, slot in enumerate((first, 2, 3)):
            other = nbr_ref[0, slot]
            wanted = jnp.where(
                (other // members == panel) & (slot < count_ref[0]),
                lax.rem(other, members) + k * members,
                -1,
            )
            hot = jnp.where(asked_row == wanted, 1.0, hot)
        return hot

    centres[0:BLOCK, :] = features
    centres[BLOCK:ROWS, :] = place
    centres[ROWS:, :] = slots_in(2 * core, core)
    asked[1, 0:BLOCK, :] = features
    asked[1, BLOCK:ROWS, :] = place
    asked[1, ROWS : ROWS + 3 * members, :] = slots_in(1, 1 - core)
    asked[1, ROWS + 3 * members :, :] = slots_in(2 - 2 * core, 1 - core)
    asked[0, ROWS + 3 * members :, :] = jnp.zeros((3 * members, C), F32)

    @pl.when(core == 1)
    def _():
        pl.semaphore_wait(barrier, 2 * members)
        pl.semaphore_signal(group_sem, inc=1, device_id=(sib_slab, me), device_id_type=MESH)

    @pl.when(core == 0)
    def _():
        pl.semaphore_wait(group_sem, 1)

    def arrival(member, to=me):
        return pltpu.make_async_remote_copy(
            src_ref=own.at[member],
            dst_ref=own.at[member],
            send_sem=own_send_sem,
            recv_sem=own_recv_sem.at[member],
            device_id=(slab, to),
            device_id_type=MESH,
        )

    def lend(member):
        return pltpu.make_async_remote_copy(
            src_ref=own.at[member],
            dst_ref=near.at[member],
            send_sem=near_send_sem,
            recv_sem=near_recv_sem.at[member],
            device_id=(sib_slab, me),
            device_id_type=MESH,
        )

    for mate in mates:
        arrival(me, mate).start()
    lend(me).start()

    def copy(index, source, target, to_slab):
        return pltpu.make_async_remote_copy(
            src_ref=source,
            dst_ref=target,
            send_sem=send_sem.at[index],
            recv_sem=recv_sem.at[index],
            device_id=(to_slab, me),
            device_id_type=MESH,
        )

    ask = copy(0, centres, asked.at[0, pl.ds(0, ROWS + 3 * members)], far_slab)
    tell = copy(1, centre_sums.at[0], returned, far_slab)
    repay = copy(2, near_grads, near_back, sib_slab)
    early = slab == 0

    def ask_far():
        @pl.when(core == 0)
        def _():
            pl.semaphore_wait(barrier, 1)

        ask.start()

    pl.when(jnp.logical_not(early))(ask_far)

    atom = lax.broadcasted_iota(jnp.int32, (BLOCK, CHUNK), 0)
    lane = lax.broadcasted_iota(jnp.int32, (BLOCK, CHUNK), 1)
    hot_j = jnp.where(lax.rem(lane, BLOCK) == atom, 1.0, 0.0).astype(F32)
    rhs_pair[...] = jnp.concatenate([hot_j, hot_j], axis=0).astype(BF16)
    hot_i = centre_onehot(0, CHUNK)[0:CENTRES]
    rhs_centre[...] = jnp.concatenate([hot_i, hot_i], axis=0).astype(BF16)
    for load in loads[7:]:
        load.wait()
    radial_hi, radial_lo = parts(radial_ref[...], 2)
    lhs_r[...] = (jnp.concatenate([radial_hi, radial_lo], axis=0) * 0.25).astype(BF16)
    lhs_m[...] = (wmix_ref[...].astype(F32).T * 0.5).astype(BF16)
    ones = jnp.ones((16, C), F32)
    lhs_b[...] = jnp.concatenate(
        [
            jnp.concatenate([jnp.zeros((C, C), F32), ones], axis=0),
            jnp.concatenate([wmix_ref[...].astype(F32), jnp.zeros((16, C), F32)], axis=0),
        ],
        axis=1,
    ).astype(BF16)
    readout = readout_ref[...].reshape(1, C)
    ro_exp[...] = jnp.broadcast_to(readout, (C, C)).T
    grads[...] = jnp.zeros_like(grads)
    near_sum[...] = jnp.zeros_like(near_sum)

    row8 = lax.broadcasted_iota(jnp.int32, (8, BLOCK), 0)
    center = lax.broadcasted_iota(jnp.int32, (8, CHUNK), 0).astype(F32) * ROOT
    line = lax.broadcasted_iota(jnp.int32, (ROWS_OF_PAIRS, BLOCK), 0)
    atom = lax.broadcasted_iota(jnp.int32, (ROWS_OF_PAIRS, BLOCK), 1)
    on_line = jnp.where(atom // 2 == line, 1.0, 0.0)
    lane = lax.broadcasted_iota(jnp.int32, (BLOCK, C), 1)
    atom = lax.broadcasted_iota(jnp.int32, (BLOCK, C), 0)
    in_half = jnp.where(lax.rem(atom, 2) == lane // BLOCK, 1.0, 0.0).astype(BF16)
    line = lax.broadcasted_iota(jnp.int32, (ROWS_OF_PAIRS, C), 0)
    lane = lax.broadcasted_iota(jnp.int32, (ROWS_OF_PAIRS, C), 1)
    same_atom = jnp.where(2 * line + lane // BLOCK == lax.rem(lane, BLOCK), 1.0, 0.0)
    mates_blocks = own.at[pl.ds(0, members - 1)]
    mates_grads = grads.at[pl.ds(0, members - 1)]

    for mate in mates:
        arrival(mate).wait_recv()
        lend(mate).start()
    pl.when(early)(ask_far)

    def group(turn, carry):
        which = jnp.where(early, 1 - turn, turn)

        @pl.when(which == 0)
        def _():
            ask.wait_recv()
            near_used[...] = jnp.zeros_like(near_used)

        @pl.when(which == 1)
        def _():
            for block in range(members):
                lend(block).wait_recv()
            near_used[...] = near[...]

        spot = asked[which, BLOCK:ROWS, 0:BLOCK]
        scale8 = jnp.zeros((8, BLOCK), F32)
        for r in range(4):
            for s in range(4):
                there = (row8 == s) & (spot[3:4] == float(r))
                scale8 = jnp.where(there, scale_ref[r, s], scale8)
        wide = []
        for values in [spot[k : k + 1] for k in range(3)] + [scale8[k : k + 1] for k in range(4)]:
            wide += [on_line * part for part in parts(values, 3)]
        found = dot(jnp.concatenate(wide, axis=0).astype(BF16), in_half)
        for k in range(7):
            base = k * 3 * ROWS_OF_PAIRS
            one, two, three = (
                found[base + p * ROWS_OF_PAIRS : base + (p + 1) * ROWS_OF_PAIRS] for p in range(3)
            )
            spread[k] = one + two + three
        half_hi, half_lo = parts(radial_ref[...] * 0.5, 2)
        for k in range(PAIRS // CHUNK):
            mine = pl.ds(k * CENTRES, CENTRES)
            self_hi, self_lo = parts(asked[which, mine, :] * 0.5, 2)
            rest = [half_hi, half_lo, half_hi, jnp.zeros((8, C), F32), self_hi, self_lo]
            lhs_rest[k] = jnp.concatenate(rest, axis=0).T.astype(BF16)
        pair_acc[...] = jnp.zeros_like(pair_acc)

        def begin(slot):
            hot_rows = pl.ds(ROWS + slot * members, members)
            near_rows = pl.ds(ROWS + (slot + 3) * members, members)
            hot = asked[which, hot_rows, :]
            near_hot = asked[which, near_rows, :]
            live = jnp.sum(hot + near_hot, axis=0, keepdims=True)
            self_hot = asked[which, pl.ds(ROWS + slot * members + me, 1), :]
            self_hot = jnp.where(which == 1, self_hot, 0.0)
            block = own[0] * hot[0:1] + near_used[0] * near_hot[0:1]
            for k in range(1, members):
                block = block + own[k] * hot[k : k + 1] + near_used[k] * near_hot[k : k + 1]
            lhs_send[slot] = jnp.concatenate(parts(block[0:BLOCK] * 0.5, 2), axis=0).T.astype(BF16)
            place_j = block[BLOCK:ROWS, 0:BLOCK]
            place_j = jnp.concatenate([place_j, place_j], axis=1)
            diff = [place_j[k : k + 1] - spread[k] for k in range(3)]
            dist_sq = diff[0] * diff[0] + diff[1] * diff[1] + diff[2] * diff[2]
            kind = place_j[3:4]
            scale = jnp.where(
                kind == 0.0,
                spread[3],
                jnp.where(kind == 1.0, spread[4], jnp.where(kind == 2.0, spread[5], spread[6])),
            )
            scaled = dist_sq * scale
            scaled_ref[slot] = scaled * (ROOT / SPACING)
            keep = live - self_hot * same_atom
            reach = jnp.maximum(1.0 - scaled * (1.0 / 2.5), 0.0)
            return hot, near_hot, diff, scale, keep, reach

        def first(slot, turn):
            base = turn * (CHUNK // C)
            wide = [scaled_ref[slot, base + k : base + k + 1, :] for k in range(CHUNK // C)]
            offset = jnp.concatenate(wide, axis=1) - center
            basis = jnp.exp2(-(offset * offset))
            slope = basis * offset
            basis_hi, basis_lo = parts(basis, 2)
            head = jnp.concatenate(
                [basis_hi, basis_hi, basis_lo, jnp.zeros((8, CHUNK), F32)], axis=0
            ).astype(BF16)
            rhs = jnp.concatenate([rhs_pair[...], head, rhs_centre[...]], axis=0)
            lhs = jnp.concatenate([lhs_send[slot], lhs_rest[turn]], axis=1)
            return slot, base, slope, dot(lhs, rhs)

        def second(state):
            half = state[-1]
            t = jnp.tanh(half)
            p = 1.0 + t
            hidden = half * p
            slope_1 = p + hidden * (1.0 - t)
            half = dot(lhs_m[...], hidden.astype(BF16))
            return state[:-1] + (slope_1, half)

        def third(state):
            half = state[-1]
            t = jnp.tanh(half)
            p = (1.0 + t) * jnp.concatenate([ro_exp[...]] * (CHUNK // C), axis=1)
            mixed = half * p
            mixed = mixed.astype(BF16)
            slope_2 = p.astype(BF16) + mixed * (1.0 - t.astype(BF16))
            out = dot(lhs_b[...], jnp.concatenate([mixed, slope_2], axis=0))
            return state[:-1] + (out,)

        def fourth(state):
            slot, base, slope, slope_1, out = state
            d_basis = dot(lhs_r[...], (out[0:C] * slope_1).astype(BF16))
            slope = jnp.sum((d_basis[0:8] + d_basis[8:16]) * slope, axis=0, keepdims=True)
            for k in range(CHUNK // C):
                lanes = slice(k * C, (k + 1) * C)
                slope_ref[slot, base + k : base + k + 1, :] = slope[:, lanes]
                energy_rows[slot, base + k : base + k + 1, :] = out[C : C + 1, lanes]

        def finish(slot, known):
            hot, near_hot, diff, scale, keep, reach = known
            energy = energy_rows[slot]
            cut = reach * reach
            d_scaled = cut * slope_ref[slot] * (-2.0 / (SPACING * ROOT))
            d_scaled = 2.0 * keep * scale * (d_scaled - (2.0 / 2.5) * reach * energy)
            found = [d_scaled * part for part in diff]
            for k in range(3):
                pair_acc[k] += found[k]
            pair_acc[3] += keep * cut * energy
            total = [jnp.sum(part, axis=0, keepdims=True) for part in found]
            total = jnp.concatenate(total + [jnp.zeros((5, C), F32)], axis=0)
            grad = total[:, 0:BLOCK] + total[:, BLOCK:C]
            grad = jnp.concatenate([grad, jnp.zeros_like(grad)], axis=1)
            for k in range(members):
                grads[k] += grad * hot[k : k + 1]
                near_sum[k] += grad * near_hot[k : k + 1]

        stages = [first, second, third, fourth]
        count = PAIRS // CHUNK
        known, states = {}, {}
        for turn in range(3 * count + 3):
            for depth in range(4):
                sub = turn - depth
                if not 0 <= sub < 3 * count:
                    continue
                slot, part = divmod(sub, count)
                if depth == 0:
                    if sub == 0:
                        known[0] = begin(0)
                    if part == count - 1 and slot < 2:
                        known[slot + 1] = begin(slot + 1)
                    states[sub] = first(slot, part)
                else:
                    states[sub] = stages[depth](states[sub])
                if depth == 3 and part == count - 1:
                    finish(slot, known.pop(slot))

        wide = []
        for k in range(4):
            wide += parts(pair_acc[k], 3)
        found = lax.dot_general(
            jnp.concatenate(wide, axis=0).astype(BF16),
            in_half,
            (((1,), (1,)), ((), ())),
            preferred_element_type=F32,
        )
        total = []
        for k in range(4):
            base = k * 3 * ROWS_OF_PAIRS
            one, two, three = (
                found[base + p * ROWS_OF_PAIRS : base + (p + 1) * ROWS_OF_PAIRS] for p in range(3)
            )
            total.append(jnp.sum((one + two + three) * on_line, axis=0, keepdims=True))
        total = jnp.concatenate(total + [jnp.zeros((4, BLOCK), F32)], axis=0)
        centre_sums[which] = jnp.concatenate([total, jnp.zeros_like(total)], axis=1)

        @pl.when(which == 0)
        def _():
            tell.start()

        @pl.when(which == 1)
        def _():
            near_grads[...] = near_sum[...]
            repay.start()

        return carry

    lax.fori_loop(0, 2, group, 0)

    repay.wait_recv()
    grads[...] += near_back[...]
    for mate in mates:
        pltpu.make_async_remote_copy(
            src_ref=grads.at[mate],
            dst_ref=back.at[me],
            send_sem=back_send_sem,
            recv_sem=back_recv_sem,
            device_id=(slab, mate),
            device_id_type=MESH,
        ).start()
    back[me] = grads[me]

    tell.wait_recv()
    centre_sum = centre_sums[1] + returned[...]
    energy_ref[...] = centre_sum[3:4, 0:BLOCK].reshape(BLOCK)
    pltpu.make_async_copy(mates_grads, mates_grads, back_recv_sem).wait()
    total = back[0]
    for k in range(1, members):
        total = total + back[k]
    force_ref[...] = (centre_sum - total)[0:3, 0:BLOCK]

    for sent in (ask, tell, repay):
        sent.wait_send()
    pltpu.make_async_copy(near, near, near_send_sem).wait()
    pltpu.make_async_copy(mates_blocks, mates_blocks, own_send_sem).wait()
    pltpu.make_async_copy(mates_grads, mates_grads, back_send_sem).wait()


def solution(mesh):
    slabs, members = mesh.shape["slab"], mesh.shape["grp"]
    vmem = pl.BlockSpec(memory_space=pltpu.VMEM)
    call = pl.pallas_call(
        functools.partial(kernel, slabs, members),
        out_shape=(
            jax.ShapeDtypeStruct((BLOCK,), F32),
            jax.ShapeDtypeStruct((3, BLOCK), F32),
        ),
        in_specs=[pl.BlockSpec(memory_space=pltpu.HBM)] * 11,
        out_specs=(vmem, vmem),
        scratch_shapes=[
            pltpu.VMEM((3, BLOCK), F32),
            pltpu.VMEM((BLOCK,), jnp.int32),
            pltpu.VMEM((BLOCK, C), BF16),
            pltpu.VMEM((C, C), BF16),
            pltpu.VMEM((C, C), BF16),
            pltpu.VMEM((8, C), F32),
            pltpu.VMEM((C, C), BF16),
            pltpu.VMEM((C,), F32),
            pltpu.SMEM((4, 4), F32),
            pltpu.SMEM((1, 4), jnp.int32),
            pltpu.SMEM((1,), jnp.int32),
            pltpu.VMEM((members, ROWS, C), F32),
            pltpu.VMEM((members, ROWS, C), F32),
            pltpu.VMEM((members, ROWS, C), F32),
            pltpu.VMEM((2, ROWS + 6 * members, C), F32),
            pltpu.VMEM((ROWS + 3 * members, C), F32),
            pltpu.VMEM((7, ROWS_OF_PAIRS, C), F32),
            pltpu.VMEM((3, ROWS_OF_PAIRS, C), F32),
            pltpu.VMEM((3, ROWS_OF_PAIRS, C), F32),
            pltpu.VMEM((3, ROWS_OF_PAIRS, C), F32),
            pltpu.VMEM((2 * BLOCK, CHUNK), BF16),
            pltpu.VMEM((2 * CENTRES, CHUNK), BF16),
            pltpu.VMEM((3, C, 2 * BLOCK), BF16),
            pltpu.VMEM((PAIRS // CHUNK, C, 32 + 2 * CENTRES), BF16),
            pltpu.VMEM((C + 16, 2 * C), BF16),
            pltpu.VMEM((16, C), BF16),
            pltpu.VMEM((C, C), BF16),
            pltpu.VMEM((C, C), F32),
            pltpu.VMEM((4, ROWS_OF_PAIRS, C), F32),
            pltpu.VMEM((2, 8, C), F32),
            pltpu.VMEM((members, 8, C), F32),
            pltpu.VMEM((members, 8, C), F32),
            pltpu.VMEM((members, 8, C), F32),
            pltpu.VMEM((members, 8, C), F32),
            pltpu.VMEM((8, C), F32),
            pltpu.VMEM((members, 8, C), F32),
            pltpu.SemaphoreType.DMA((11,)),
            pltpu.SemaphoreType.DMA((3,)),
            pltpu.SemaphoreType.DMA((3,)),
            pltpu.SemaphoreType.DMA,
            pltpu.SemaphoreType.DMA((members,)),
            pltpu.SemaphoreType.DMA,
            pltpu.SemaphoreType.DMA((members,)),
            pltpu.SemaphoreType.DMA,
            pltpu.SemaphoreType.DMA,
            pltpu.SemaphoreType.REGULAR,
        ],
        compiler_params=pltpu.CompilerParams(
            collective_id=0, has_side_effects=True, vmem_limit_bytes=60 * 2**20
        ),
    )
    return jax.shard_map(
        call,
        mesh=mesh,
        in_specs=(
            P(None, ("slab", "grp")),
            P(("slab", "grp")),
            P(("slab", "grp"), None),
            P(),
            P(),
            P(),
            P(),
            P(),
            P(),
            P(("slab", "grp"), None),
            P(("slab", "grp")),
        ),
        out_specs=(P(("slab", "grp")), P(None, ("slab", "grp"))),
        check_vma=False,
    )
```
